256 devices in a mesh: layer: 32 (over z, x_lo, core), dp: 8 (over y, x_hi).
Axes of the slice: x: 4 (x_hi: 2, x_lo: 2; x = x_hi * 2 + x_lo), y: 4, z: 8, core: 2. Of those that a mesh axis runs over, the one named last changes fastest.
Arguments:
- weights: float32 [64, 1024, 1024], P('layer', 'dp'), may hold values from -6 to 6
- momentum: float32 [64, 1024, 1024], P('layer', 'dp'), may hold values from -3 to 3
- boundary: float32 [32, 2048, 1024], P('layer', 'dp'), may hold values from -6 to 6
- adjoint: float32 [32, 2048, 1024], P('layer', 'dp'), may hold values from -6 to 6
- target: float32 [2048, 1024], P('dp'), may hold values from -6 to 6
Outputs:
- new_weights: float32 [64, 1024, 1024], P('layer', 'dp')
- new_momentum: float32 [64, 1024, 1024], P('layer', 'dp')
- new_boundary: float32 [32, 2048, 1024], P('layer', 'dp')
- new_adjoint: float32 [32, 2048, 1024], P('layer', 'dp')
The draws below stay inside these ranges and needn't reach their ends.
All inputs are finite; a program needn't handle non-finite values.
Results may differ from the reference program's by a relative error of at most 0.012.
Values may be sent and summed in bfloat16 or wider, within the bound.
No kernel may reach another device: no remote copies, remote signals or barrier semaphores. Data moves between devices by JAX's collectives and lax.ppermute only.
A program may use at most 64 MiB of HBM per device.

```python
import math
import jax
import jax.numpy as jnp
from jax import lax

D = 1024
LPD = 2
STEPS = 2
SWEEPS = 2
GROUPS = 32
LAYERS = 64
ROWS = 2048


def block_levels(key, shape, shards, smallest, high):
    loudness = 1.0
    for axis_at, blocks in shards:
        draws = jax.random.uniform(jax.random.fold_in(jax.random.fold_in(key, 6), axis_at), (blocks,), jnp.float32, smallest / len(shards), high / len(shards))
        loudness = loudness * jnp.repeat(jnp.exp(draws), shape[axis_at] // blocks).reshape((-1,) + (1,) * (len(shape) - 1 - axis_at))
    return loudness


def noise(key, extent, deviation, bound, split=(), kind=jnp.bfloat16):
    loudness = block_levels(key, extent, split, -0.22, 0.18) if split else 1.0
    values = jax.random.normal(key, extent, jnp.float32) * deviation * loudness
    return jnp.minimum(jnp.maximum(values, -bound), bound).astype(kind)


def setup_inputs(seed: int = 0) -> dict:
    seeds = jax.random.split(jax.random.key(seed), 6)
    weights = noise(seeds[0], (LAYERS, D, D), 1.0, 6.0, ((0, 32), (1, 8)), jnp.float32)
    momentum = noise(seeds[1], (LAYERS, D, D), 0.5, 3.0, ((0, 32), (1, 8)), jnp.float32)
    boundary = noise(seeds[2], (GROUPS, ROWS, D), 1.0, 6.0, ((0, 32), (1, 8)), jnp.float32)
    adjoint = noise(seeds[3], (GROUPS, ROWS, D), 1.0, 6.0, ((0, 32), (1, 8)), jnp.float32)
    target = noise(seeds[4], (ROWS, D), 1.0, 6.0, ((0, 8),), jnp.float32)
    return dict(weights=weights, momentum=momentum, boundary=boundary, adjoint=adjoint, target=target)


step_size = 0.5
momentum_decay = 0.9
learn_rate = 0.05

def forward_all(current, rounded_weights, width_scale):
    inputs_list = []
    slopes_list = []
    for layer_at in range(LPD):
        rounded = current.astype(jnp.bfloat16)
        product = jnp.einsum('grd,gde->gre', rounded.astype(jnp.float32), rounded_weights[:, layer_at].astype(jnp.float32), precision=lax.Precision.HIGHEST)
        squashed = jnp.tanh(product * width_scale)
        current = current + step_size * squashed
        inputs_list.append(rounded)
        slopes_list.append(squashed)
    return (current, inputs_list, slopes_list)

def backward_all(cotangent, rounded_weights, slopes_list, width_scale):
    for layer_at in reversed(range(LPD)):
        slope = slopes_list[layer_at]
        signal = (cotangent * (1.0 - slope * slope)).astype(jnp.bfloat16)
        pulled = jnp.einsum('gre,gde->grd', signal.astype(jnp.float32), rounded_weights[:, layer_at].astype(jnp.float32), precision=lax.Precision.HIGHEST)
        cotangent = cotangent + step_size * width_scale * pulled
    return cotangent

def gradient_all(cotangent, rounded_weights, inputs_list, slopes_list, width_scale, row_scale):
    grads = [None] * LPD
    for layer_at in reversed(range(LPD)):
        slope = slopes_list[layer_at]
        signal = (cotangent * (1.0 - slope * slope)).astype(jnp.bfloat16)
        grads[layer_at] = jnp.einsum('grd,gre->gde', inputs_list[layer_at].astype(jnp.float32), signal.astype(jnp.float32), precision=lax.Precision.HIGHEST) * row_scale
        if layer_at > 0:
            pulled = jnp.einsum('gre,gde->grd', signal.astype(jnp.float32), rounded_weights[:, layer_at].astype(jnp.float32), precision=lax.Precision.HIGHEST)
            cotangent = cotangent + step_size * width_scale * pulled
    return jnp.stack(grads, axis=1).reshape(LAYERS, D, D)

def reference(weights, momentum, boundary, adjoint, target):
    width_scale = 1.0 / math.sqrt(D)
    row_scale = 1.0 / math.sqrt(ROWS)
    current = boundary
    cotangent = adjoint
    for update_at in range(STEPS):
        rounded_weights = weights.astype(jnp.bfloat16).reshape(GROUPS, LPD, D, D)
        for sweep_at in range(SWEEPS):
            finals, inputs_list, slopes_list = forward_all(current, rounded_weights, width_scale)
            current = jnp.concatenate([current[:1], finals[:-1]], axis=0)
        finals, inputs_list, slopes_list = forward_all(current, rounded_weights, width_scale)
        missing = finals[-1] - target
        for sweep_at in range(SWEEPS):
            starts = backward_all(cotangent, rounded_weights, slopes_list, width_scale)
            cotangent = jnp.concatenate([starts[1:], missing[None]], axis=0)
        grads = gradient_all(cotangent, rounded_weights, inputs_list, slopes_list, width_scale, row_scale)
        momentum = momentum_decay * momentum + grads
        weights = weights - learn_rate * momentum
    return (weights, momentum, current, cotangent)
```

```python
import math

import jax
import jax.numpy as jnp
from jax import lax
from jax.sharding import PartitionSpec as P

STEPS = 2
SWEEPS = 2


step_size = 0.5
momentum_decay = 0.9
learn_rate = 0.05
HALVES = 2


def passed_along(value, axis, by):
    devices = lax.axis_size(axis)
    pairs = [(i, i + by) for i in range(devices) if 0 <= i + by < devices]
    return lax.ppermute(value, axis, pairs)


def turned(value, by):
    shards = lax.axis_size("dp")
    return lax.ppermute(value, "dp", [(i, (i + HALVES * by) % shards) for i in range(shards)])


def swapped(value):
    shards = lax.axis_size("dp")
    return lax.ppermute(value, "dp", [(i, i ^ 1) for i in range(shards)])


def place(turns, across):
    shards = lax.axis_size("dp")
    own = lax.axis_index("dp")
    return lax.rem(own + HALVES * turns + shards, shards) ^ across


def gather_weights(own):
    layers, rows, width = own.shape
    other = swapped(own)
    before = turned(own, 1)
    after = turned(own, -1)
    far_first = turned(before[:1], 1)
    far_second = turned(after[1:], -1)
    other_before = turned(other, 1)
    other_after = turned(other, -1)
    other_far_first = swapped(far_first)
    other_far_second = swapped(far_second)
    full = jnp.zeros((layers, rows * lax.axis_size("dp"), width), own.dtype)

    def put(full, piece, turns, across, layer_at=0):
        return lax.dynamic_update_slice(full, piece, (layer_at, place(turns, across) * rows, 0))

    full = put(full, own, 0, 0)
    full = put(full, other, 0, 1)
    full = put(full, before, -1, 0)
    full = put(full, after, 1, 0)
    full = put(full, far_first, 2, 0)
    full = put(full, far_second, 2, 0, 1)
    full = put(full, other_before, -1, 1)
    full = put(full, other_after, 1, 1)
    full = put(full, other_far_first, 2, 1)
    full = put(full, other_far_second, 2, 1, 1)
    return full


def scatter_sum(terms):
    shards = lax.axis_size("dp")
    width = terms[0].shape[1]
    rows = terms[0].shape[0] // shards

    def block(layer_at, turns, across):
        return lax.dynamic_slice(terms[layer_at], (place(turns, across) * rows, 0), (rows, width))

    def blocks(turns, across):
        return jnp.stack([block(k, turns, across) for k in range(2)])

    def add(*values):
        total = values[0].astype(jnp.float32)
        for value in values[1:]:
            total = total + value.astype(jnp.float32)
        return total

    far_other = swapped(blocks(2, 1))
    from_before = turned(blocks(1, 1), 1)
    from_after = turned(blocks(-1, 1), -1)
    far_first = turned(add(block(0, 2, 0), far_other[0]).astype(jnp.bfloat16), 1)
    far_second = turned(add(block(1, 2, 0), far_other[1]).astype(jnp.bfloat16), -1)
    across = swapped(add(blocks(0, 1), from_before, from_after).astype(jnp.bfloat16))
    onward = jnp.stack([add(block(0, 1, 0), far_first).astype(jnp.bfloat16), block(1, 1, 0)])
    back = jnp.stack([block(0, -1, 0), add(block(1, -1, 0), far_second).astype(jnp.bfloat16)])
    from_onward = turned(onward, 1)
    from_back = turned(back, -1)
    return add(blocks(0, 0), across, from_onward, from_back)


def forward_group(current, full_weights, width_scale):
    inputs_list = []
    slopes_list = []
    for layer_at in range(full_weights.shape[0]):
        rounded = current.astype(jnp.bfloat16)
        product = jnp.dot(rounded, full_weights[layer_at], preferred_element_type=jnp.float32)
        squashed = jnp.tanh(product * width_scale)
        current = current + step_size * squashed
        inputs_list.append(rounded)
        slopes_list.append(squashed)
    return (current, inputs_list, slopes_list)


def pull_back(signal, matrix):
    return lax.dot_general(
        signal, matrix, (((1,), (1,)), ((), ())), preferred_element_type=jnp.float32
    )


def backward_group(cotangent, full_weights, slopes_list, width_scale):
    for layer_at in reversed(range(len(slopes_list))):
        slope = slopes_list[layer_at]
        signal = (cotangent * (1.0 - slope * slope)).astype(jnp.bfloat16)
        cotangent = cotangent + step_size * width_scale * pull_back(signal, full_weights[layer_at])
    return cotangent


def outer_rows(left, right):
    return lax.dot_general(
        left, right, (((0,), (0,)), ((), ())), preferred_element_type=jnp.float32
    )


def local(weights, momentum, boundary, adjoint, target):
    groups = lax.axis_size("layer")
    group_at = lax.axis_index("layer")
    shards = lax.axis_size("dp")
    width = weights.shape[2]
    width_scale = 1.0 / math.sqrt(width)
    row_scale = 1.0 / math.sqrt(boundary.shape[1] * shards)
    is_first = group_at == 0
    is_last = group_at == groups - 1
    current_in = boundary[0]
    cotangent_in = adjoint[0]
    for update_at in range(STEPS):
        full_weights = gather_weights(weights.astype(jnp.bfloat16))
        for sweep_at in range(SWEEPS):
            outgoing = forward_group(current_in, full_weights, width_scale)[0]
            received = passed_along(outgoing.astype(jnp.bfloat16), "layer", 1)
            current_in = jnp.where(is_first, current_in, received.astype(jnp.float32))
        finals, inputs_list, slopes_list = forward_group(current_in, full_weights, width_scale)
        missing = finals - target
        for sweep_at in range(SWEEPS):
            starting = backward_group(cotangent_in, full_weights, slopes_list, width_scale)
            received = passed_along(starting.astype(jnp.bfloat16), "layer", -1)
            cotangent_in = jnp.where(is_last, missing, received.astype(jnp.float32))
        cotangent = cotangent_in
        terms = [None] * len(slopes_list)
        for layer_at in reversed(range(len(slopes_list))):
            slope = slopes_list[layer_at]
            signal = (cotangent * (1.0 - slope * slope)).astype(jnp.bfloat16)
            terms[layer_at] = outer_rows(inputs_list[layer_at], signal).astype(jnp.bfloat16)
            if layer_at > 0:
                cotangent = cotangent + step_size * width_scale * pull_back(
                    signal, full_weights[layer_at]
                )
        momentum = momentum_decay * momentum + scatter_sum(terms) * row_scale
        weights = weights - learn_rate * momentum
    return (weights, momentum, current_in[None], cotangent_in[None])


def solution(mesh):
    placed = (
        P("layer", "dp", None),
        P("layer", "dp", None),
        P("layer", "dp", None),
        P("layer", "dp", None),
        P("dp", None),
    )
    return jax.shard_map(
        local,
        mesh=mesh,
        in_specs=placed,
        out_specs=(
            P("layer", "dp", None),
            P("layer", "dp", None),
            P("layer", "dp", None),
            P("layer", "dp", None),
        ),
        check_vma=False,
    )
```

```python
import functools
import math

import jax
import jax.numpy as jnp
from jax import lax
from jax.experimental import pallas as pl
from jax.experimental.pallas import tpu as pltpu
from jax.sharding import PartitionSpec as P

STEPS = 2
SWEEPS = 2


step_size = 0.5
momentum_decay = 0.9
learn_rate = 0.05
HALVES = 2
F32 = jnp.float32
BF16 = jnp.bfloat16


def passed_along(value, axis, by):
    devices = lax.axis_size(axis)
    pairs = [(i, i + by) for i in range(devices) if 0 <= i + by < devices]
    return lax.ppermute(value, axis, pairs)


def turned(value, by):
    shards = lax.axis_size("dp")
    return lax.ppermute(value, "dp", [(i, (i + HALVES * by) % shards) for i in range(shards)])


def swapped(value):
    shards = lax.axis_size("dp")
    return lax.ppermute(value, "dp", [(i, i ^ 1) for i in range(shards)])


def on_device(body, outs, operands, flops=0):
    whole = pl.BlockSpec(memory_space=pltpu.VMEM)
    shapes = [jax.ShapeDtypeStruct(shape, kind) for shape, kind in outs]
    moved = sum(math.prod(o.shape) * o.dtype.itemsize for o in [*operands, *shapes])
    return pl.pallas_call(
        body,
        out_shape=shapes,
        in_specs=[whole] * len(operands),
        out_specs=[whole] * len(shapes),
        cost_estimate=pl.CostEstimate(flops=flops, bytes_accessed=moved, transcendentals=0),
        compiler_params=pltpu.CompilerParams(vmem_limit_bytes=20 * 2**20),
    )(*operands)


def rows_of(at, turns, across, rows, shards):
    place = lax.rem(at + HALVES * turns + shards, shards)
    if across:
        place = place + 1 - 2 * lax.rem(place, 2)
    return pl.ds(pl.multiple_of(place * rows, rows), rows)


def first_group():
    return lax.axis_index("layer") == 0


def last_group():
    return lax.axis_index("layer") == lax.axis_size("layer") - 1


def times(left, right):
    return jnp.dot(left, right, preferred_element_type=F32)


def pull_back(signal, matrix):
    return lax.dot_general(signal, matrix, (((1,), (1,)), ((), ())), preferred_element_type=F32)


def outer_rows(left, right):
    return lax.dot_general(left, right, (((0,), (0,)), ((), ())), preferred_element_type=F32)


def round_kernel(weights, both, first, second):
    rounded = weights[...].astype(BF16)
    both[...] = rounded
    first[...] = rounded[0]
    second[...] = rounded[1]


def layers_forward(current, full, width_scale, inputs=(), bends=()):
    for layer_at in range(full.shape[0]):
        rounded = current.astype(BF16)
        squashed = jnp.tanh(times(rounded, full[layer_at]) * width_scale)
        current = current + step_size * squashed
        if inputs:
            inputs[layer_at][...] = rounded
            bends[layer_at][...] = 1.0 - squashed * squashed
    return current


def layers_backward(cotangent, full, bends, width_scale):
    for layer_at in reversed(range(full.shape[0])):
        signal = (cotangent * bends[layer_at][...]).astype(BF16)
        cotangent = cotangent + step_size * width_scale * pull_back(signal, full[layer_at])
    return cotangent


def first_forward_kernel(width_scale, shards, *refs):
    at = lax.axis_index("dp")
    pieces, (kept, received, full, outgoing) = refs[:-4], refs[-4:]
    own, other, b0, b1, a0, a1, f0, f1, other_before, other_after, z0, z1 = pieces
    rows = own.shape[1]
    for layer_at in range(2):
        def put(piece, turns, across):
            full[layer_at, rows_of(at, turns, across, rows, shards)] = piece

        put(own[layer_at], 0, False)
        put(other[layer_at], 0, True)
        put((b0, b1)[layer_at][...], -1, False)
        put((a0, a1)[layer_at][...], 1, False)
        put((f0, f1)[layer_at][...], 2, False)
        put(other_before[layer_at], -1, True)
        put(other_after[layer_at], 1, True)
        put((z0, z1)[layer_at][...], 2, True)
    current = jnp.where(first_group(), kept[...], received[...].astype(F32))
    outgoing[...] = layers_forward(current, full, width_scale).astype(BF16)


def forward_kernel(width_scale, kept, received, full, outgoing):
    current = jnp.where(first_group(), kept[...], received[...].astype(F32))
    outgoing[...] = layers_forward(current, full, width_scale).astype(BF16)


def turn_kernel(width_scale, kept, received, full, target, ending, arrived,
                current_in, missing, input_0, input_1, bend_0, bend_1, starting):
    current = jnp.where(first_group(), kept[...], received[...].astype(F32))
    current_in[...] = current
    bends = (bend_0, bend_1)
    finals = layers_forward(current, full, width_scale, (input_0, input_1), bends)
    missing[...] = finals - target[...]
    cotangent = jnp.where(last_group(), ending[...], arrived[...].astype(F32))
    starting[...] = layers_backward(cotangent, full, bends, width_scale).astype(BF16)


def backward_kernel(width_scale, missing, received, full, bend_0, bend_1, starting):
    cotangent = jnp.where(last_group(), missing[...], received[...].astype(F32))
    starting[...] = layers_backward(cotangent, full, (bend_0, bend_1), width_scale).astype(BF16)


def gradient_kernel(width_scale, shards, missing, received, full, input_0, input_1, bend_0, bend_1,
                    cotangent_in, fx0, fx1, ux, dx, f0, f1, ox, u0, u1, d0, d1, own, terms):
    at = lax.axis_index("dp")
    cotangent = jnp.where(last_group(), missing[...], received[...].astype(F32))
    cotangent_in[...] = cotangent
    signal = (cotangent * bend_1[...]).astype(BF16)
    terms[1] = outer_rows(input_1[...], signal).astype(BF16)
    cotangent = cotangent + step_size * width_scale * pull_back(signal, full[1])
    signal = (cotangent * bend_0[...]).astype(BF16)
    terms[0] = outer_rows(input_0[...], signal).astype(BF16)
    rows = terms.shape[1] // shards
    for layer_at in range(2):
        def block(turns, across):
            return terms[layer_at, rows_of(at, turns, across, rows, shards)]

        (fx0, fx1)[layer_at][...] = block(2, True)
        ux[layer_at] = block(1, True)
        dx[layer_at] = block(-1, True)
        (f0, f1)[layer_at][...] = block(2, False)
        ox[layer_at] = block(0, True)
        (u0, u1)[layer_at][...] = block(1, False)
        (d0, d1)[layer_at][...] = block(-1, False)
        own[layer_at] = block(0, False)


def add_kernel(*refs):
    total = refs[0][...].astype(F32)
    for ref in refs[1:-1]:
        total = total + ref[...].astype(F32)
    refs[-1][...] = total.astype(BF16)


def added(*values):
    return on_device(add_kernel, [(values[0].shape, BF16)], values)[0]


def update_kernel(row_scale, weights, momentum, own, across, u0, u1, d0, d1,
                  new_weights, new_momentum, both, first, second):
    for layer_at in range(2):
        total = own[layer_at].astype(F32) + across[layer_at].astype(F32)
        total = total + (u0, u1)[layer_at][...].astype(F32)
        total = total + (d0, d1)[layer_at][...].astype(F32)
        moved = momentum_decay * momentum[layer_at] + total * row_scale
        new_momentum[layer_at] = moved
        stepped = weights[layer_at] - learn_rate * moved
        new_weights[layer_at] = stepped
        rounded = stepped.astype(BF16)
        both[layer_at] = rounded
        (first, second)[layer_at][...] = rounded


def gather_pieces(both, first, second):
    b0 = turned(first, 1)
    a1 = turned(second, -1)
    other = swapped(both)
    f0 = turned(b0, 1)
    f1 = turned(a1, -1)
    b1 = turned(second, 1)
    a0 = turned(first, -1)
    z0 = swapped(f0)
    z1 = swapped(f1)
    return both, other, b0, b1, a0, a1, f0, f1, turned(other, 1), turned(other, -1), z0, z1


def local(weights, momentum, boundary, adjoint, target):
    shards = lax.axis_size("dp")
    layers, own_rows, width = weights.shape
    rows = boundary.shape[1]
    width_scale = 1.0 / math.sqrt(width)
    row_scale = 1.0 / math.sqrt(rows * shards)
    state = (rows, width)
    shard = (layers, own_rows, width)
    block = (own_rows, width)
    product = 2 * rows * width * width
    kept = boundary[0]
    received = kept
    ending = adjoint[0]
    arrived = ending
    own = on_device(round_kernel, [(shard, BF16), (block, BF16), (block, BF16)], (weights,))
    for update_at in range(STEPS):
        full, outgoing = on_device(
            functools.partial(first_forward_kernel, width_scale, shards),
            [((layers, width, width), BF16), (state, BF16)],
            (*gather_pieces(*own), kept, received), 2 * product,
        )
        received = passed_along(outgoing, "layer", 1)
        outgoing = on_device(
            functools.partial(forward_kernel, width_scale),
            [(state, BF16)], (kept, received, full), 2 * product,
        )[0]
        received = passed_along(outgoing, "layer", 1)
        current_in, missing, input_0, input_1, bend_0, bend_1, starting = on_device(
            functools.partial(turn_kernel, width_scale),
            [(state, F32)] * 2 + [(state, BF16)] * 2 + [(state, F32)] * 2 + [(state, BF16)],
            (kept, received, full, target, ending, arrived), 4 * product,
        )
        ending = missing
        arrived = passed_along(starting, "layer", -1)
        starting = on_device(
            functools.partial(backward_kernel, width_scale),
            [(state, BF16)], (missing, arrived, full, bend_0, bend_1), 2 * product,
        )[0]
        arrived = passed_along(starting, "layer", -1)
        cotangent_in, fx0, fx1, ux, dx, f0, f1, ox, u0, u1, d0, d1, mine, _ = on_device(
            functools.partial(gradient_kernel, width_scale, shards),
            [(state, F32), (block, BF16), (block, BF16), (shard, BF16), (shard, BF16), (block, BF16),
             (block, BF16), (shard, BF16)] + [(block, BF16)] * 4 + [(shard, BF16), ((layers, width, width), BF16)],
            (missing, arrived, full, input_0, input_1, bend_0, bend_1), 3 * product,
        )
        from_far_0 = swapped(fx0)
        from_far_1 = swapped(fx1)
        before = turned(ux, 1)
        after = turned(dx, -1)
        relay_0 = turned(added(f0, from_far_0), 1)
        relay_1 = turned(added(f1, from_far_1), -1)
        up_1 = turned(u1, 1)
        down_0 = turned(d0, -1)
        across = swapped(added(ox, before, after))
        up_0 = turned(added(u0, relay_0), 1)
        down_1 = turned(added(d1, relay_1), -1)
        weights, momentum, *own = on_device(
            functools.partial(update_kernel, row_scale),
            [(shard, F32), (shard, F32), (shard, BF16), (block, BF16), (block, BF16)],
            (weights, momentum, mine, across, up_0, up_1, down_0, down_1),
        )
    return (weights, momentum, current_in[None], cotangent_in[None])


def solution(mesh):
    placed = (
        P("layer", "dp", None),
        P("layer", "dp", None),
        P("layer", "dp", None),
        P("layer", "dp", None),
        P("dp", None),
    )
    return jax.shard_map(
        local,
        mesh=mesh,
        in_specs=placed,
        out_specs=(
            P("layer", "dp", None),
            P("layer", "dp", None),
            P("layer", "dp", None),
            P("layer", "dp", None),
        ),
        check_vma=False,
    )
```

```python
import functools
import math

import jax
import jax.numpy as jnp
from jax import lax
from jax.experimental import pallas as pl
from jax.experimental.pallas import tpu as pltpu
from jax.sharding import PartitionSpec as P

STEPS = 2
SWEEPS = 2


step_size = 0.5
momentum_decay = 0.9
learn_rate = 0.05
HALVES = 2
F32 = jnp.float32
BF16 = jnp.bfloat16


def passed_along(value, axis, by):
    devices = lax.axis_size(axis)
    pairs = [(i, i + by) for i in range(devices) if 0 <= i + by < devices]
    return lax.ppermute(value, axis, pairs)


def turned(value, by):
    shards = lax.axis_size("dp")
    return lax.ppermute(value, "dp", [(i, (i + HALVES * by) % shards) for i in range(shards)])


def swapped(value):
    shards = lax.axis_size("dp")
    return lax.ppermute(value, "dp", [(i, i ^ 1) for i in range(shards)])


def on_device(body, outs, operands, flops=0):
    whole = pl.BlockSpec(memory_space=pltpu.VMEM)
    shapes = [jax.ShapeDtypeStruct(shape, kind) for shape, kind in outs]
    moved = sum(math.prod(o.shape) * o.dtype.itemsize for o in [*operands, *shapes])
    return pl.pallas_call(
        body,
        out_shape=shapes,
        in_specs=[whole] * len(operands),
        out_specs=[whole] * len(shapes),
        cost_estimate=pl.CostEstimate(flops=flops, bytes_accessed=moved, transcendentals=0),
        compiler_params=pltpu.CompilerParams(vmem_limit_bytes=20 * 2**20),
    )(*operands)


def rows_of(at, turns, across, rows, shards):
    place = lax.rem(at + HALVES * turns + shards, shards)
    if across:
        place = place + 1 - 2 * lax.rem(place, 2)
    return pl.ds(pl.multiple_of(place * rows, rows), rows)


def times(left, right):
    return jnp.dot(left, right, preferred_element_type=F32)


def pull_back(signal, matrix):
    return lax.dot_general(signal, matrix, (((1,), (1,)), ((), ())), preferred_element_type=F32)


def round_kernel(weights, both, first, second):
    rounded = weights[...].astype(BF16)
    both[...] = rounded
    first[...] = rounded[0]
    second[...] = rounded[1]


def layers_forward(current, full, width_scale, inputs=(), bends=()):
    for layer_at in range(full.shape[0]):
        rounded = current.astype(BF16)
        squashed = jnp.tanh(times(rounded, full[layer_at]) * width_scale)
        current = current + step_size * squashed
        if inputs:
            inputs[layer_at][...] = rounded
            bends[layer_at][...] = 1.0 - squashed * squashed
    return current


def layers_backward(cotangent, full, bends, width_scale):
    for layer_at in reversed(range(full.shape[0])):
        signal = (cotangent * bends[layer_at][...]).astype(BF16)
        cotangent = cotangent + step_size * width_scale * pull_back(signal, full[layer_at])
    return cotangent


def half_of(ref, half):
    rows = ref.shape[0] // 2
    return ref[half * rows:(half + 1) * rows]


def entering(kept, received, half):
    own = half_of(kept, half)
    if received is None:
        return own
    return jnp.where(lax.axis_index("layer") == 0, own, received[...].astype(F32))


def turning(missing, arrived):
    last = lax.axis_index("layer") == lax.axis_size("layer") - 1
    return jnp.where(last, missing[...], arrived[...].astype(F32))


def assemble_kernel(shards, *refs):
    own, other, b0, b1, a0, a1, f0, f1, other_before, other_after, z0, z1, full = refs
    at = lax.axis_index("dp")
    rows = own.shape[1]
    for layer_at in range(2):
        def put(piece, turns, across):
            full[layer_at, rows_of(at, turns, across, rows, shards)] = piece

        put(own[layer_at], 0, False)
        put(other[layer_at], 0, True)
        put((b0, b1)[layer_at][...], -1, False)
        put((a0, a1)[layer_at][...], 1, False)
        put((f0, f1)[layer_at][...], 2, False)
        put(other_before[layer_at], -1, True)
        put(other_after[layer_at], 1, True)
        put((z0, z1)[layer_at][...], 2, True)


def forward_kernel(width_scale, half, pieces, fresh, *refs):
    *joined, kept = refs[:pieces + 1]
    refs = refs[pieces + 1:]
    received = None if fresh else refs[0]
    refs = refs if fresh else refs[1:]
    if pieces:
        full, outgoing = refs
        assemble_kernel(lax.axis_size("dp"), *joined, full)
    else:
        full, outgoing = refs
    outgoing[...] = layers_forward(entering(kept, received, half), full, width_scale).astype(BF16)


def turn_kernel(width_scale, half, fresh, kept, received, full, target, *refs):
    if fresh:
        adjoint, *refs = refs
        cotangent = half_of(adjoint, half)
    else:
        ending, arrived, *refs = refs
        cotangent = turning(ending, arrived)
    missing, input_0, input_1, bend_0, bend_1, starting = refs
    bends = (bend_0, bend_1)
    finals = layers_forward(entering(kept, received, half), full, width_scale, (input_0, input_1), bends)
    missing[...] = finals - half_of(target, half)
    starting[...] = layers_backward(cotangent, full, bends, width_scale).astype(BF16)


def backward_kernel(width_scale, missing, arrived, full, bend_0, bend_1, starting):
    cotangent = turning(missing, arrived)
    starting[...] = layers_backward(cotangent, full, (bend_0, bend_1), width_scale).astype(BF16)


def flip_kernel(*refs):
    halves, outs = refs[:4], refs[4:]
    for layer_at in range(2):
        for half in range(2):
            piece = halves[2 * layer_at + half]
            rows = piece.shape[0]
            outs[layer_at][:, half * rows:(half + 1) * rows] = piece[...].T


def block_of(flipped, signal, at, turns, across, shards):
    rows = flipped.shape[0] // shards
    return times(flipped[rows_of(at, turns, across, rows, shards)], signal[...]).astype(BF16)


def far_gradient_kernel(width_scale, shards, missing_a, missing_b, arrived_a, arrived_b, full, flipped_0, flipped_1,
                        bend_0a, bend_0b, bend_1a, bend_1b, fx0, fx1, ux, dx, signal_0, signal_1):
    at = lax.axis_index("dp")
    cotangent = jnp.concatenate([turning(missing_a, arrived_a), turning(missing_b, arrived_b)])
    signal_1[...] = (cotangent * jnp.concatenate([bend_1a[...], bend_1b[...]])).astype(BF16)
    cotangent = cotangent + step_size * width_scale * pull_back(signal_1[...], full[1])
    signal_0[...] = (cotangent * jnp.concatenate([bend_0a[...], bend_0b[...]])).astype(BF16)
    fx0[...] = block_of(flipped_0, signal_0, at, 2, True, shards)
    fx1[...] = block_of(flipped_1, signal_1, at, 2, True, shards)
    for layer_at, flipped, signal in ((0, flipped_0, signal_0), (1, flipped_1, signal_1)):
        ux[layer_at] = block_of(flipped, signal, at, 1, True, shards)
        dx[layer_at] = block_of(flipped, signal, at, -1, True, shards)


def near_gradient_kernel(shards, flipped_0, flipped_1, signal_0, signal_1, f0, f1, ox, u0, u1, d0, d1, own):
    at = lax.axis_index("dp")
    for layer_at, flipped, signal in ((0, flipped_0, signal_0), (1, flipped_1, signal_1)):
        (f0, f1)[layer_at][...] = block_of(flipped, signal, at, 2, False, shards)
        ox[layer_at] = block_of(flipped, signal, at, 0, True, shards)
        (u0, u1)[layer_at][...] = block_of(flipped, signal, at, 1, False, shards)
        (d0, d1)[layer_at][...] = block_of(flipped, signal, at, -1, False, shards)
        own[layer_at] = block_of(flipped, signal, at, 0, False, shards)


def settle_kernel(kept, received_a, received_b, missing_a, missing_b, arrived_a, arrived_b, current_in, cotangent_in):
    rows = received_a.shape[0]
    for half, received, missing, arrived in ((0, received_a, missing_a, arrived_a), (1, received_b, missing_b, arrived_b)):
        current_in[half * rows:(half + 1) * rows] = entering(kept, received, half)
        cotangent_in[half * rows:(half + 1) * rows] = turning(missing, arrived)


def add_kernel(*refs):
    total = refs[0][...].astype(F32)
    for ref in refs[1:-1]:
        total = total + ref[...].astype(F32)
    refs[-1][...] = total.astype(BF16)


def added(*values):
    return on_device(add_kernel, [(values[0].shape, BF16)], values)[0]


def update_kernel(row_scale, weights, momentum, own, across, u0, u1, d0, d1,
                  new_weights, new_momentum, both, first, second):
    for layer_at in range(2):
        total = own[layer_at].astype(F32) + across[layer_at].astype(F32)
        total = total + (u0, u1)[layer_at][...].astype(F32)
        total = total + (d0, d1)[layer_at][...].astype(F32)
        moved = momentum_decay * momentum[layer_at] + total * row_scale
        new_momentum[layer_at] = moved
        stepped = weights[layer_at] - learn_rate * moved
        new_weights[layer_at] = stepped
        rounded = stepped.astype(BF16)
        both[layer_at] = rounded
        (first, second)[layer_at][...] = rounded


def gather_pieces(both, first, second):
    b0 = turned(first, 1)
    a1 = turned(second, -1)
    other = swapped(both)
    f0 = turned(b0, 1)
    f1 = turned(a1, -1)
    b1 = turned(second, 1)
    a0 = turned(first, -1)
    z0 = swapped(f0)
    z1 = swapped(f1)
    return both, other, b0, b1, a0, a1, f0, f1, turned(other, 1), turned(other, -1), z0, z1


def local(weights, momentum, boundary, adjoint, target):
    shards = lax.axis_size("dp")
    layers, own_rows, width = weights.shape
    rows = boundary.shape[1]
    width_scale = 1.0 / math.sqrt(width)
    row_scale = 1.0 / math.sqrt(rows * shards)
    half_state = (rows // 2, width)
    state = (rows, width)
    shard = (layers, own_rows, width)
    block = (own_rows, width)
    whole = (layers, width, width)
    product = rows * width * width
    kept = boundary[0]
    received = [None, None]
    ending = adjoint[0]
    own = on_device(round_kernel, [(shard, BF16), (block, BF16), (block, BF16)], (weights,))
    for update_at in range(STEPS):
        fresh = update_at == 0
        pieces = gather_pieces(*own)
        for sweep_at in range(SWEEPS):
            for half in range(2):
                joined = pieces if sweep_at == 0 and half == 0 else ()
                outs = [(half_state, BF16)]
                operands = [*joined, kept]
                if received[half] is not None:
                    operands.append(received[half])
                if joined:
                    outs = [(whole, BF16), *outs]
                else:
                    operands.append(full)
                body = functools.partial(forward_kernel, width_scale, half, len(joined), received[half] is None)
                *made, outgoing = on_device(body, outs, operands, 2 * product)
                if made:
                    full = made[0]
                received[half] = passed_along(outgoing, "layer", 1)
        turned_out = []
        for half in range(2):
            before = (ending,) if fresh else (turned_last[half][0], arrived[half])
            turned_out.append(on_device(
                functools.partial(turn_kernel, width_scale, half, fresh),
                [(half_state, F32)] + [(half_state, BF16)] * 2 + [(half_state, F32)] * 2 + [(half_state, BF16)],
                (kept, received[half], full, target, *before), 4 * product,
            ))
        arrived = [passed_along(turned_out[half][5], "layer", -1) for half in range(2)]
        turned_last = turned_out
        missing = [turned_out[half][0] for half in range(2)]
        bends = [turned_out[half][3 + layer_at] for layer_at in range(2) for half in range(2)]
        flipped = on_device(
            flip_kernel, [((width, rows), BF16)] * 2,
            [turned_out[half][1 + layer_at] for layer_at in range(2) for half in range(2)],
        )
        for sweep_at in range(SWEEPS - 1):
            for half in range(2):
                starting = on_device(
                    functools.partial(backward_kernel, width_scale), [(half_state, BF16)],
                    (missing[half], arrived[half], full, bends[half], bends[2 + half]), 2 * product,
                )[0]
                arrived[half] = passed_along(starting, "layer", -1)
        fx0, fx1, ux, dx, *signals = on_device(
            functools.partial(far_gradient_kernel, width_scale, shards),
            [(block, BF16), (block, BF16), (shard, BF16), (shard, BF16), (state, BF16), (state, BF16)],
            (*missing, *arrived, full, *flipped, *bends), 4 * product,
        )
        f0, f1, ox, u0, u1, d0, d1, mine = on_device(
            functools.partial(near_gradient_kernel, shards),
            [(block, BF16), (block, BF16), (shard, BF16)] + [(block, BF16)] * 4 + [(shard, BF16)],
            (*flipped, *signals), 2 * product,
        )
        from_far_0 = swapped(fx0)
        from_far_1 = swapped(fx1)
        before = turned(ux, 1)
        after = turned(dx, -1)
        relay_0 = turned(added(f0, from_far_0), 1)
        relay_1 = turned(added(f1, from_far_1), -1)
        up_1 = turned(u1, 1)
        down_0 = turned(d0, -1)
        across = swapped(added(ox, before, after))
        up_0 = turned(added(u0, relay_0), 1)
        down_1 = turned(added(d1, relay_1), -1)
        weights, momentum, *own = on_device(
            functools.partial(update_kernel, row_scale),
            [(shard, F32), (shard, F32), (shard, BF16), (block, BF16), (block, BF16)],
            (weights, momentum, mine, across, up_0, up_1, down_0, down_1),
        )
    current_in, cotangent_in = on_device(settle_kernel, [(state, F32)] * 2, (kept, *received, *missing, *arrived))
    return (weights, momentum, current_in[None], cotangent_in[None])


def solution(mesh):
    placed = (
        P("layer", "dp", None),
        P("layer", "dp", None),
        P("layer", "dp", None),
        P("layer", "dp", None),
        P("dp", None),
    )
    return jax.shard_map(
        local,
        mesh=mesh,
        in_specs=placed,
        out_specs=(
            P("layer", "dp", None),
            P("layer", "dp", None),
            P("layer", "dp", None),
            P("layer", "dp", None),
        ),
        check_vma=False,
    )
```

```python
import functools
import math

import jax
import jax.numpy as jnp
from jax import lax
from jax.experimental import pallas as pl
from jax.experimental.pallas import tpu as pltpu
from jax.sharding import PartitionSpec as P

STEPS = 2
SWEEPS = 2


step_size = 0.5
momentum_decay = 0.9
learn_rate = 0.05
HALVES = 2
F32 = jnp.float32
BF16 = jnp.bfloat16


def passed(value, by, crossing):
    groups = lax.axis_size("layer")
    pairs = [(i, i + by) for i in range(groups) if 0 <= i + by < groups]
    return lax.ppermute(value, "layer", [(i, j) for i, j in pairs if (i // 2 != j // 2) == crossing])


def turned(value, by):
    shards = lax.axis_size("dp")
    return lax.ppermute(value, "dp", [(i, (i + HALVES * by) % shards) for i in range(shards)])


def swapped(value):
    shards = lax.axis_size("dp")
    return lax.ppermute(value, "dp", [(i, i ^ 1) for i in range(shards)])


def on_device(body, outs, operands, flops=0):
    whole = pl.BlockSpec(memory_space=pltpu.VMEM)
    shapes = [jax.ShapeDtypeStruct(shape, kind) for shape, kind in outs]
    moved = sum(math.prod(o.shape) * o.dtype.itemsize for o in [*operands, *shapes])
    return pl.pallas_call(
        body,
        out_shape=shapes,
        in_specs=[whole] * len(operands),
        out_specs=[whole] * len(shapes),
        cost_estimate=pl.CostEstimate(flops=flops, bytes_accessed=moved, transcendentals=0),
        compiler_params=pltpu.CompilerParams(vmem_limit_bytes=20 * 2**20),
    )(*operands)


def rows_of(at, turns, across, rows, shards):
    place = lax.rem(at + HALVES * turns + shards, shards)
    if across:
        place = place + 1 - 2 * lax.rem(place, 2)
    return pl.ds(pl.multiple_of(place * rows, rows), rows)


def times(left, right):
    return jnp.dot(left, right, preferred_element_type=F32)


def pull_back(signal, matrix):
    return lax.dot_general(signal, matrix, (((1,), (1,)), ((), ())), preferred_element_type=F32)


def round_kernel(weights, both, first, second):
    rounded = weights[...].astype(BF16)
    both[...] = rounded
    first[...] = rounded[0]
    second[...] = rounded[1]


def layers_forward(current, full, width_scale, inputs=(), bends=()):
    for layer_at in range(full.shape[0]):
        rounded = current.astype(BF16)
        squashed = jnp.tanh(times(rounded, full[layer_at]) * width_scale)
        current = current + step_size * squashed
        if inputs:
            inputs[layer_at][...] = rounded
            bends[layer_at][...] = 1.0 - squashed * squashed
    return current


def layers_backward(cotangent, full, bends, width_scale):
    for layer_at in reversed(range(full.shape[0])):
        signal = (cotangent * bends[layer_at][...]).astype(BF16)
        cotangent = cotangent + step_size * width_scale * pull_back(signal, full[layer_at])
    return cotangent


def entering(kept, within, crossed):
    at = lax.axis_index("layer")
    arrived = jnp.where(lax.rem(at, 2) == 1, within[...], crossed[...])
    return jnp.where(at == 0, kept[...], arrived.astype(F32))


def turning(missing, within, crossed):
    at = lax.axis_index("layer")
    arrived = jnp.where(lax.rem(at, 2) == 0, within[...], crossed[...])
    return jnp.where(at == lax.axis_size("layer") - 1, missing[...], arrived.astype(F32))


def assemble_kernel(shards, *refs):
    own, other, b0, b1, a0, a1, f0, f1, other_before, other_after, z0, z1, full = refs
    at = lax.axis_index("dp")
    rows = own.shape[1]
    for layer_at in range(2):
        def put(piece, turns, across):
            full[layer_at, rows_of(at, turns, across, rows, shards)] = piece

        put(own[layer_at], 0, False)
        put(other[layer_at], 0, True)
        put((b0, b1)[layer_at][...], -1, False)
        put((a0, a1)[layer_at][...], 1, False)
        put((f0, f1)[layer_at][...], 2, False)
        put(other_before[layer_at], -1, True)
        put(other_after[layer_at], 1, True)
        put((z0, z1)[layer_at][...], 2, True)


def first_forward_kernel(width_scale, fresh, *refs):
    pieces, kept, refs = refs[:12], refs[12], refs[13:]
    current = kept[...] if fresh else entering(kept, *refs[:2])
    full, outgoing = refs[-2:]
    assemble_kernel(lax.axis_size("dp"), *pieces, full)
    outgoing[...] = layers_forward(current, full, width_scale).astype(BF16)


def within_forward_kernel(width_scale, received, full, outgoing):
    outgoing[...] = layers_forward(received[...].astype(F32), full, width_scale).astype(BF16)


def crossed_forward_kernel(width_scale, kept, received, full, outgoing):
    current = jnp.where(lax.axis_index("layer") == 0, kept[...], received[...].astype(F32))
    outgoing[...] = layers_forward(current, full, width_scale).astype(BF16)


def turn_kernel(width_scale, fresh, kept, within, crossed, full, target, *refs):
    if fresh:
        adjoint, *refs = refs
        cotangent = adjoint[...]
    else:
        ending, within_back, crossed_back, *refs = refs
        cotangent = turning(ending, within_back, crossed_back)
    missing, input_0, input_1, bend_0, bend_1, starting = refs
    bends = (bend_0, bend_1)
    finals = layers_forward(entering(kept, within, crossed), full, width_scale, (input_0, input_1), bends)
    missing[...] = finals - target[...]
    starting[...] = layers_backward(cotangent, full, bends, width_scale).astype(BF16)


def within_backward_kernel(width_scale, received, full, bend_0, bend_1, starting):
    starting[...] = layers_backward(received[...].astype(F32), full, (bend_0, bend_1), width_scale).astype(BF16)


def crossed_backward_kernel(width_scale, missing, received, full, bend_0, bend_1, starting):
    last = lax.axis_index("layer") == lax.axis_size("layer") - 1
    cotangent = jnp.where(last, missing[...], received[...].astype(F32))
    starting[...] = layers_backward(cotangent, full, (bend_0, bend_1), width_scale).astype(BF16)


def flip_kernel(input_0, input_1, flipped_0, flipped_1):
    flipped_0[...] = input_0[...].T
    flipped_1[...] = input_1[...].T


def block_of(flipped, signal, at, turns, across, shards):
    rows = flipped.shape[0] // shards
    return times(flipped[rows_of(at, turns, across, rows, shards)], signal[...]).astype(BF16)


def far_gradient_kernel(width_scale, shards, missing, within, crossed, full, flipped_0, flipped_1, bend_0, bend_1,
                        fx0, fx1, ux, dx, signal_0, signal_1):
    at = lax.axis_index("dp")
    cotangent = turning(missing, within, crossed)
    signal_1[...] = (cotangent * bend_1[...]).astype(BF16)
    cotangent = cotangent + step_size * width_scale * pull_back(signal_1[...], full[1])
    signal_0[...] = (cotangent * bend_0[...]).astype(BF16)
    fx0[...] = block_of(flipped_0, signal_0, at, 2, True, shards)
    fx1[...] = block_of(flipped_1, signal_1, at, 2, True, shards)
    for layer_at, flipped, signal in ((0, flipped_0, signal_0), (1, flipped_1, signal_1)):
        ux[layer_at] = block_of(flipped, signal, at, 1, True, shards)
        dx[layer_at] = block_of(flipped, signal, at, -1, True, shards)


def near_gradient_kernel(shards, flipped_0, flipped_1, signal_0, signal_1, f0, f1, ox, u0, u1, d0, d1, own):
    at = lax.axis_index("dp")
    for layer_at, flipped, signal in ((0, flipped_0, signal_0), (1, flipped_1, signal_1)):
        (f0, f1)[layer_at][...] = block_of(flipped, signal, at, 2, False, shards)
        ox[layer_at] = block_of(flipped, signal, at, 0, True, shards)
        (u0, u1)[layer_at][...] = block_of(flipped, signal, at, 1, False, shards)
        (d0, d1)[layer_at][...] = block_of(flipped, signal, at, -1, False, shards)
        own[layer_at] = block_of(flipped, signal, at, 0, False, shards)


def settle_kernel(kept, within, crossed, missing, within_back, crossed_back, current_in, cotangent_in):
    current_in[...] = entering(kept, within, crossed)
    cotangent_in[...] = turning(missing, within_back, crossed_back)


def add_kernel(*refs):
    total = refs[0][...].astype(F32)
    for ref in refs[1:-1]:
        total = total + ref[...].astype(F32)
    refs[-1][...] = total.astype(BF16)


def added(*values):
    return on_device(add_kernel, [(values[0].shape, BF16)], values)[0]


def update_kernel(row_scale, weights, momentum, own, across, u0, u1, d0, d1,
                  new_weights, new_momentum, both, first, second):
    for layer_at in range(2):
        total = own[layer_at].astype(F32) + across[layer_at].astype(F32)
        total = total + (u0, u1)[layer_at][...].astype(F32)
        total = total + (d0, d1)[layer_at][...].astype(F32)
        moved = momentum_decay * momentum[layer_at] + total * row_scale
        new_momentum[layer_at] = moved
        stepped = weights[layer_at] - learn_rate * moved
        new_weights[layer_at] = stepped
        rounded = stepped.astype(BF16)
        both[layer_at] = rounded
        (first, second)[layer_at][...] = rounded


def gather_pieces(both, first, second):
    b0 = turned(first, 1)
    a1 = turned(second, -1)
    other = swapped(both)
    f0 = turned(b0, 1)
    f1 = turned(a1, -1)
    b1 = turned(second, 1)
    a0 = turned(first, -1)
    z0 = swapped(f0)
    z1 = swapped(f1)
    return both, other, b0, b1, a0, a1, f0, f1, turned(other, 1), turned(other, -1), z0, z1


def local(weights, momentum, boundary, adjoint, target):
    shards = lax.axis_size("dp")
    layers, own_rows, width = weights.shape
    rows = boundary.shape[1]
    width_scale = 1.0 / math.sqrt(width)
    row_scale = 1.0 / math.sqrt(rows * shards)
    state = (rows, width)
    shard = (layers, own_rows, width)
    block = (own_rows, width)
    whole = (layers, width, width)
    product = rows * width * width
    kept = boundary[0]
    entered = ()
    returned = (adjoint[0],)
    own = on_device(round_kernel, [(shard, BF16), (block, BF16), (block, BF16)], (weights,))
    for update_at in range(STEPS):
        fresh = update_at == 0
        full, outgoing = on_device(
            functools.partial(first_forward_kernel, width_scale, fresh), [(whole, BF16), (state, BF16)],
            (*gather_pieces(*own), kept, *entered), 4 * product,
        )
        crossed = passed(outgoing, 1, True)
        within = passed(outgoing, 1, False)
        from_within = on_device(
            functools.partial(within_forward_kernel, width_scale), [(state, BF16)], (within, full), 4 * product,
        )[0]
        crossed_last = passed(from_within, 1, True)
        from_crossed = on_device(
            functools.partial(crossed_forward_kernel, width_scale), [(state, BF16)], (kept, crossed, full), 4 * product,
        )[0]
        entered = (passed(from_crossed, 1, False), crossed_last)
        missing, input_0, input_1, bend_0, bend_1, starting = on_device(
            functools.partial(turn_kernel, width_scale, fresh),
            [(state, F32)] + [(state, BF16)] * 2 + [(state, F32)] * 2 + [(state, BF16)],
            (kept, *entered, full, target, *returned), 8 * product,
        )
        bends = (bend_0, bend_1)
        crossed = passed(starting, -1, True)
        within = passed(starting, -1, False)
        flipped = on_device(flip_kernel, [((width, rows), BF16)] * 2, (input_0, input_1))
        from_within = on_device(
            functools.partial(within_backward_kernel, width_scale), [(state, BF16)], (within, full, *bends), 4 * product,
        )[0]
        crossed_last = passed(from_within, -1, True)
        from_crossed = on_device(
            functools.partial(crossed_backward_kernel, width_scale), [(state, BF16)],
            (missing, crossed, full, *bends), 4 * product,
        )[0]
        returned = (missing, passed(from_crossed, -1, False), crossed_last)
        fx0, fx1, ux, dx, *signals = on_device(
            functools.partial(far_gradient_kernel, width_scale, shards),
            [(block, BF16), (block, BF16), (shard, BF16), (shard, BF16), (state, BF16), (state, BF16)],
            (*returned, full, *flipped, *bends), 4 * product,
        )
        f0, f1, ox, u0, u1, d0, d1, mine = on_device(
            functools.partial(near_gradient_kernel, shards),
            [(block, BF16), (block, BF16), (shard, BF16)] + [(block, BF16)] * 4 + [(shard, BF16)],
            (*flipped, *signals), 2 * product,
        )
        from_far_0 = swapped(fx0)
        from_far_1 = swapped(fx1)
        before = turned(ux, 1)
        after = turned(dx, -1)
        relay_0 = turned(added(f0, from_far_0), 1)
        relay_1 = turned(added(f1, from_far_1), -1)
        up_1 = turned(u1, 1)
        down_0 = turned(d0, -1)
        across = swapped(added(ox, before, after))
        up_0 = turned(added(u0, relay_0), 1)
        down_1 = turned(added(d1, relay_1), -1)
        weights, momentum, *own = on_device(
            functools.partial(update_kernel, row_scale),
            [(shard, F32), (shard, F32), (shard, BF16), (block, BF16), (block, BF16)],
            (weights, momentum, mine, across, up_0, up_1, down_0, down_1),
        )
    current_in, cotangent_in = on_device(settle_kernel, [(state, F32)] * 2, (kept, *entered, *returned))
    return (weights, momentum, current_in[None], cotangent_in[None])


def solution(mesh):
    placed = (
        P("layer", "dp", None),
        P("layer", "dp", None),
        P("layer", "dp", None),
        P("layer", "dp", None),
        P("dp", None),
    )
    return jax.shard_map(
        local,
        mesh=mesh,
        in_specs=placed,
        out_specs=(
            P("layer", "dp", None),
            P("layer", "dp", None),
            P("layer", "dp", None),
            P("layer", "dp", None),
        ),
        check_vma=False,
    )
```

```python
import functools
import math

import jax
import jax.numpy as jnp
from jax import lax
from jax.experimental import pallas as pl
from jax.experimental.pallas import tpu as pltpu
from jax.sharding import PartitionSpec as P

STEPS = 2
SWEEPS = 2


step_size = 0.5
momentum_decay = 0.9
learn_rate = 0.05
HALVES = 2
F32 = jnp.float32
BF16 = jnp.bfloat16


def passed(value, by, crossing):
    groups = lax.axis_size("layer")
    pairs = [(i, i + by) for i in range(groups) if 0 <= i + by < groups]
    return lax.ppermute(value, "layer", [(i, j) for i, j in pairs if (i // 2 != j // 2) == crossing])


def turned(value, by):
    shards = lax.axis_size("dp")
    return lax.ppermute(value, "dp", [(i, (i + HALVES * by) % shards) for i in range(shards)])


def swapped(value):
    shards = lax.axis_size("dp")
    return lax.ppermute(value, "dp", [(i, i ^ 1) for i in range(shards)])


def on_device(body, outs, operands, flops=0, in_place=None):
    whole = pl.BlockSpec(memory_space=pltpu.VMEM)
    shapes = [jax.ShapeDtypeStruct(shape, kind) for shape, kind in outs]
    moved = sum(math.prod(o.shape) * o.dtype.itemsize for o in [*operands, *shapes])
    return pl.pallas_call(
        body,
        out_shape=shapes,
        in_specs=[whole] * len(operands),
        out_specs=[whole] * len(shapes),
        input_output_aliases=in_place or {},
        cost_estimate=pl.CostEstimate(flops=flops, bytes_accessed=moved, transcendentals=0),
        compiler_params=pltpu.CompilerParams(vmem_limit_bytes=20 * 2**20),
    )(*operands)


def rows_of(at, turns, across, rows, shards):
    place = lax.rem(at + HALVES * turns + shards, shards)
    if across:
        place = place + 1 - 2 * lax.rem(place, 2)
    return pl.ds(pl.multiple_of(place * rows, rows), rows)


def times(left, right):
    return jnp.dot(left, right, preferred_element_type=F32)


def pull_back(signal, matrix):
    return lax.dot_general(signal, matrix, (((1,), (1,)), ((), ())), preferred_element_type=F32)


def round_kernel(weights, both, first, second):
    rounded = weights[...].astype(BF16)
    both[...] = rounded
    first[...] = rounded[0]
    second[...] = rounded[1]


def layers_forward(current, full, width_scale, inputs=(), bends=()):
    for layer_at in range(full.shape[0]):
        rounded = current.astype(BF16)
        squashed = jnp.tanh(times(rounded, full[layer_at]) * width_scale)
        current = current + step_size * squashed
        if inputs:
            inputs[layer_at][...] = rounded
            bends[layer_at][...] = 1.0 - squashed * squashed
    return current


def layers_backward(cotangent, full, bends, width_scale):
    for layer_at in reversed(range(full.shape[0])):
        signal = (cotangent * bends[layer_at][...]).astype(BF16)
        cotangent = cotangent + step_size * width_scale * pull_back(signal, full[layer_at])
    return cotangent


def entering(kept, within, crossed):
    at = lax.axis_index("layer")
    arrived = jnp.where(lax.rem(at, 2) == 1, within[...], crossed[...])
    return jnp.where(at == 0, kept[...], arrived.astype(F32))


def turning(missing, within, crossed):
    at = lax.axis_index("layer")
    arrived = jnp.where(lax.rem(at, 2) == 0, within[...], crossed[...])
    return jnp.where(at == lax.axis_size("layer") - 1, missing[...], arrived.astype(F32))


def near_kernel(fresh, *refs):
    own, other, b0, b1, a0, a1, f0, f1, kept, *refs = refs
    full, far, current = refs[-3:]
    at = lax.axis_index("dp")
    shards = lax.axis_size("dp")
    rows = own.shape[1]
    for layer_at in range(2):
        def put(piece, turns, across):
            full[layer_at, rows_of(at, turns, across, rows, shards)] = piece

        put(own[layer_at], 0, False)
        put(other[layer_at], 0, True)
        put((b0, b1)[layer_at][...], -1, False)
        put((a0, a1)[layer_at][...], 1, False)
        piece = (f0, f1)[layer_at][...]
        put(piece, 2, False)
        far[layer_at] = piece
    current[...] = kept[...] if fresh else entering(kept, *refs[:2])


def first_forward_kernel(width_scale, partly, before, after, far, current, full, outgoing):
    at = lax.axis_index("dp")
    shards = lax.axis_size("dp")
    rows = far.shape[1]
    for layer_at in range(2):
        for piece, turns in ((before, -1), (after, 1), (far, 2)):
            full[layer_at, rows_of(at, turns, True, rows, shards)] = piece[layer_at]
    outgoing[...] = layers_forward(current[...], full, width_scale).astype(BF16)


def within_forward_kernel(width_scale, received, full, outgoing):
    outgoing[...] = layers_forward(received[...].astype(F32), full, width_scale).astype(BF16)


def crossed_forward_kernel(width_scale, kept, received, full, outgoing):
    current = jnp.where(lax.axis_index("layer") == 0, kept[...], received[...].astype(F32))
    outgoing[...] = layers_forward(current, full, width_scale).astype(BF16)


def turn_kernel(width_scale, fresh, kept, within, crossed, full, target, *refs):
    if fresh:
        adjoint, *refs = refs
        cotangent = adjoint[...]
    else:
        ending, within_back, crossed_back, *refs = refs
        cotangent = turning(ending, within_back, crossed_back)
    missing, input_0, input_1, bend_0, bend_1, starting = refs
    bends = (bend_0, bend_1)
    finals = layers_forward(entering(kept, within, crossed), full, width_scale, (input_0, input_1), bends)
    missing[...] = finals - target[...]
    starting[...] = layers_backward(cotangent, full, bends, width_scale).astype(BF16)


def within_backward_kernel(width_scale, received, full, bend_0, bend_1, starting):
    starting[...] = layers_backward(received[...].astype(F32), full, (bend_0, bend_1), width_scale).astype(BF16)


def crossed_backward_kernel(width_scale, missing, received, full, bend_0, bend_1, starting):
    last = lax.axis_index("layer") == lax.axis_size("layer") - 1
    cotangent = jnp.where(last, missing[...], received[...].astype(F32))
    starting[...] = layers_backward(cotangent, full, (bend_0, bend_1), width_scale).astype(BF16)


def flip_kernel(input_0, input_1, flipped_0, flipped_1):
    flipped_0[...] = input_0[...].T
    flipped_1[...] = input_1[...].T


def block_of(flipped, signal, at, turns, across, shards):
    rows = flipped.shape[0] // shards
    return times(flipped[rows_of(at, turns, across, rows, shards)], signal[...]).astype(BF16)


def far_gradient_kernel(width_scale, shards, missing, within, crossed, full, flipped_0, flipped_1, bend_0, bend_1,
                        fx, ux, dx, signal_0, signal_1):
    at = lax.axis_index("dp")
    cotangent = turning(missing, within, crossed)
    signal_1[...] = (cotangent * bend_1[...]).astype(BF16)
    cotangent = cotangent + step_size * width_scale * pull_back(signal_1[...], full[1])
    signal_0[...] = (cotangent * bend_0[...]).astype(BF16)
    for layer_at, flipped, signal in ((0, flipped_0, signal_0), (1, flipped_1, signal_1)):
        fx[layer_at] = block_of(flipped, signal, at, 2, True, shards)
        ux[layer_at] = block_of(flipped, signal, at, 1, True, shards)
        dx[layer_at] = block_of(flipped, signal, at, -1, True, shards)


def near_gradient_kernel(shards, flipped_0, flipped_1, signal_0, signal_1, far, ox, u0, u1, d0, d1, own):
    at = lax.axis_index("dp")
    for layer_at, flipped, signal in ((0, flipped_0, signal_0), (1, flipped_1, signal_1)):
        far[layer_at] = block_of(flipped, signal, at, 2, False, shards)
        ox[layer_at] = block_of(flipped, signal, at, 0, True, shards)
        (u0, u1)[layer_at][...] = block_of(flipped, signal, at, 1, False, shards)
        (d0, d1)[layer_at][...] = block_of(flipped, signal, at, -1, False, shards)
        own[layer_at] = block_of(flipped, signal, at, 0, False, shards)


def settle_kernel(kept, within, crossed, missing, within_back, crossed_back, current_in, cotangent_in):
    current_in[...] = entering(kept, within, crossed)
    cotangent_in[...] = turning(missing, within_back, crossed_back)


def sum_of(*values):
    total = values[0].astype(F32)
    for value in values[1:]:
        total = total + value.astype(F32)
    return total


def relay_kernel(far, from_far, relay_0, relay_1):
    relay_0[...] = sum_of(far[0], from_far[0]).astype(BF16)
    relay_1[...] = sum_of(far[1], from_far[1]).astype(BF16)


def across_kernel(ox, before, after, across):
    across[...] = sum_of(ox[...], before[...], after[...]).astype(BF16)


def onward_kernel(u0, relay_0, d1, relay_1, up_1, down_0, own, onward_0, back_1, partial):
    onward_0[...] = sum_of(u0[...], relay_0[...]).astype(BF16)
    back_1[...] = sum_of(d1[...], relay_1[...]).astype(BF16)
    partial[0] = sum_of(own[0], down_0[...])
    partial[1] = sum_of(own[1], up_1[...])


def update_kernel(row_scale, weights, momentum, partial, across, up_0, down_1, new_weights, new_momentum, *rounded):
    for layer_at in range(2):
        total = sum_of(partial[layer_at], across[layer_at], (up_0, down_1)[layer_at][...])
        moved = momentum_decay * momentum[layer_at] + total * row_scale
        new_momentum[layer_at] = moved
        stepped = weights[layer_at] - learn_rate * moved
        new_weights[layer_at] = stepped
        if rounded:
            rounded[0][layer_at] = stepped.astype(BF16)
            rounded[1 + layer_at][...] = stepped.astype(BF16)


def local(weights, momentum, boundary, adjoint, target):
    shards = lax.axis_size("dp")
    layers, own_rows, width = weights.shape
    rows = boundary.shape[1]
    width_scale = 1.0 / math.sqrt(width)
    row_scale = 1.0 / math.sqrt(rows * shards)
    state = (rows, width)
    shard = (layers, own_rows, width)
    block = (own_rows, width)
    whole = (layers, width, width)
    product = rows * width * width
    kept = boundary[0]
    entered = ()
    returned = (adjoint[0],)
    own = on_device(round_kernel, [(shard, BF16), (block, BF16), (block, BF16)], (weights,))
    for update_at in range(STEPS):
        fresh = update_at == 0
        both, first, second = own
        b0 = turned(first, 1)
        a1 = turned(second, -1)
        b1 = turned(second, 1)
        a0 = turned(first, -1)
        other = swapped(both)
        f0 = turned(b0, 1)
        f1 = turned(a1, -1)
        other_before = turned(other, 1)
        other_after = turned(other, -1)
        partly, far, current = on_device(
            functools.partial(near_kernel, fresh), [(whole, BF16), (shard, BF16), (state, F32)],
            (both, other, b0, b1, a0, a1, f0, f1, kept, *entered),
        )
        full, outgoing = on_device(
            functools.partial(first_forward_kernel, width_scale), [(whole, BF16), (state, BF16)],
            (partly, other_before, other_after, swapped(far), current), 4 * product, {0: 0},
        )
        crossed = passed(outgoing, 1, True)
        within = passed(outgoing, 1, False)
        from_within = on_device(
            functools.partial(within_forward_kernel, width_scale), [(state, BF16)], (within, full), 4 * product,
        )[0]
        crossed_last = passed(from_within, 1, True)
        from_crossed = on_device(
            functools.partial(crossed_forward_kernel, width_scale), [(state, BF16)], (kept, crossed, full), 4 * product,
        )[0]
        entered = (passed(from_crossed, 1, False), crossed_last)
        missing, input_0, input_1, bend_0, bend_1, starting = on_device(
            functools.partial(turn_kernel, width_scale, fresh),
            [(state, F32)] + [(state, BF16)] * 2 + [(state, F32)] * 2 + [(state, BF16)],
            (kept, *entered, full, target, *returned), 8 * product,
        )
        bends = (bend_0, bend_1)
        crossed = passed(starting, -1, True)
        within = passed(starting, -1, False)
        flipped = on_device(flip_kernel, [((width, rows), BF16)] * 2, (input_0, input_1))
        from_within = on_device(
            functools.partial(within_backward_kernel, width_scale), [(state, BF16)], (within, full, *bends), 4 * product,
        )[0]
        crossed_last = passed(from_within, -1, True)
        from_crossed = on_device(
            functools.partial(crossed_backward_kernel, width_scale), [(state, BF16)],
            (missing, crossed, full, *bends), 4 * product,
        )[0]
        returned = (missing, passed(from_crossed, -1, False), crossed_last)
        fx, ux, dx, *signals = on_device(
            functools.partial(far_gradient_kernel, width_scale, shards),
            [(shard, BF16)] * 3 + [(state, BF16)] * 2, (*returned, full, *flipped, *bends), 4 * product,
        )
        from_far = swapped(fx)
        before = turned(ux, 1)
        after = turned(dx, -1)
        far, ox, u0, u1, d0, d1, mine = on_device(
            functools.partial(near_gradient_kernel, shards),
            [(shard, BF16)] * 2 + [(block, BF16)] * 4 + [(shard, BF16)], (*flipped, *signals), 2 * product,
        )
        up_1 = turned(u1, 1)
        down_0 = turned(d0, -1)
        relay_0, relay_1 = on_device(relay_kernel, [(block, BF16)] * 2, (far, from_far))
        relay_0 = turned(relay_0, 1)
        relay_1 = turned(relay_1, -1)
        across = swapped(on_device(across_kernel, [(shard, BF16)], (ox, before, after))[0])
        onward_0, back_1, partial = on_device(
            onward_kernel, [(block, BF16)] * 2 + [(shard, F32)], (u0, relay_0, d1, relay_1, up_1, down_0, mine),
        )
        rounded = [] if update_at == STEPS - 1 else [(shard, BF16), (block, BF16), (block, BF16)]
        weights, momentum, *own = on_device(
            functools.partial(update_kernel, row_scale), [(shard, F32), (shard, F32), *rounded],
            (weights, momentum, partial, across, turned(onward_0, 1), turned(back_1, -1)),
        )
    current_in, cotangent_in = on_device(settle_kernel, [(state, F32)] * 2, (kept, *entered, *returned))
    return (weights, momentum, current_in[None], cotangent_in[None])


def solution(mesh):
    placed = (
        P("layer", "dp", None),
        P("layer", "dp", None),
        P("layer", "dp", None),
        P("layer", "dp", None),
        P("dp", None),
    )
    return jax.shard_map(
        local,
        mesh=mesh,
        in_specs=placed,
        out_specs=(
            P("layer", "dp", None),
            P("layer", "dp", None),
            P("layer", "dp", None),
            P("layer", "dp", None),
        ),
        check_vma=False,
    )
```

```python
import functools
import math

import jax
import jax.numpy as jnp
from jax import lax
from jax.experimental import pallas as pl
from jax.experimental.pallas import tpu as pltpu
from jax.sharding import PartitionSpec as P

STEPS = 2
SWEEPS = 2


step_size = 0.5
momentum_decay = 0.9
learn_rate = 0.05
HALVES = 2
F32 = jnp.float32
BF16 = jnp.bfloat16


def passed(value, by, crossing):
    groups = lax.axis_size("layer")
    pairs = [(i, i + by) for i in range(groups) if 0 <= i + by < groups]
    return lax.ppermute(value, "layer", [(i, j) for i, j in pairs if (i // 2 != j // 2) == crossing])


def turned(value, by):
    shards = lax.axis_size("dp")
    return lax.ppermute(value, "dp", [(i, (i + HALVES * by) % shards) for i in range(shards)])


def swapped(value):
    shards = lax.axis_size("dp")
    return lax.ppermute(value, "dp", [(i, i ^ 1) for i in range(shards)])


def on_device(body, outs, operands, flops=0, in_place=None):
    whole = pl.BlockSpec(memory_space=pltpu.VMEM)
    shapes = [jax.ShapeDtypeStruct(shape, kind) for shape, kind in outs]
    moved = sum(math.prod(o.shape) * o.dtype.itemsize for o in [*operands, *shapes])
    return pl.pallas_call(
        body,
        out_shape=shapes,
        in_specs=[whole] * len(operands),
        out_specs=[whole] * len(shapes),
        input_output_aliases=in_place or {},
        cost_estimate=pl.CostEstimate(flops=flops, bytes_accessed=moved, transcendentals=0),
        compiler_params=pltpu.CompilerParams(vmem_limit_bytes=20 * 2**20),
    )(*operands)


def rows_of(at, turns, across, rows, shards):
    place = lax.rem(at + HALVES * turns + shards, shards)
    if across:
        place = place + 1 - 2 * lax.rem(place, 2)
    return pl.ds(pl.multiple_of(place * rows, rows), rows)


def times(left, right):
    return jnp.dot(left, right, preferred_element_type=F32)


def pull_back(signal, matrix):
    return lax.dot_general(signal, matrix, (((1,), (1,)), ((), ())), preferred_element_type=F32)


def round_kernel(weights, both, first, second):
    rounded = weights[...].astype(BF16)
    both[...] = rounded
    first[...] = rounded[0]
    second[...] = rounded[1]


def layers_forward(current, full, width_scale, inputs=(), bends=()):
    for layer_at in range(full.shape[0]):
        rounded = current.astype(BF16)
        squashed = jnp.tanh(times(rounded, full[layer_at]) * width_scale)
        current = current + step_size * squashed
        if inputs:
            inputs[layer_at][...] = rounded
            bends[layer_at][...] = 1.0 - squashed * squashed
    return current


def layers_backward(cotangent, full, bends, width_scale):
    for layer_at in reversed(range(full.shape[0])):
        signal = (cotangent * bends[layer_at][...]).astype(BF16)
        cotangent = cotangent + step_size * width_scale * pull_back(signal, full[layer_at])
    return cotangent


def entering(kept, within, crossed):
    at = lax.axis_index("layer")
    arrived = jnp.where(lax.rem(at, 2) == 1, within[...], crossed[...])
    return jnp.where(at == 0, kept[...], arrived.astype(F32))


def turning(missing, within, crossed):
    at = lax.axis_index("layer")
    arrived = jnp.where(lax.rem(at, 2) == 0, within[...], crossed[...])
    return jnp.where(at == lax.axis_size("layer") - 1, missing[...], arrived.astype(F32))


def near_kernel(own, other, b0, b1, a0, a1, f0, f1, full, far):
    at = lax.axis_index("dp")
    shards = lax.axis_size("dp")
    rows = own.shape[1]
    for layer_at in range(2):
        def put(piece, turns, across):
            full[layer_at, rows_of(at, turns, across, rows, shards)] = piece

        put(own[layer_at], 0, False)
        put(other[layer_at], 0, True)
        put((b0, b1)[layer_at][...], -1, False)
        put((a0, a1)[layer_at][...], 1, False)
        piece = (f0, f1)[layer_at][...]
        put(piece, 2, False)
        far[layer_at] = piece


def first_forward_kernel(width_scale, partly, before, after, far, current, full, outgoing):
    at = lax.axis_index("dp")
    shards = lax.axis_size("dp")
    rows = far.shape[1]
    for layer_at in range(2):
        for piece, turns in ((before, -1), (after, 1), (far, 2)):
            full[layer_at, rows_of(at, turns, True, rows, shards)] = piece[layer_at]
    outgoing[...] = layers_forward(current[...], full, width_scale).astype(BF16)


def within_forward_kernel(width_scale, received, full, outgoing):
    outgoing[...] = layers_forward(received[...].astype(F32), full, width_scale).astype(BF16)


def crossed_forward_kernel(width_scale, kept, received, full, outgoing):
    current = jnp.where(lax.axis_index("layer") == 0, kept[...], received[...].astype(F32))
    outgoing[...] = layers_forward(current, full, width_scale).astype(BF16)


def turn_kernel(width_scale, kept, within, crossed, full, target, cotangent,
                missing, input_0, input_1, bend_0, bend_1, starting):
    bends = (bend_0, bend_1)
    finals = layers_forward(entering(kept, within, crossed), full, width_scale, (input_0, input_1), bends)
    missing[...] = finals - target[...]
    starting[...] = layers_backward(cotangent[...], full, bends, width_scale).astype(BF16)


def within_backward_kernel(width_scale, received, full, bend_0, bend_1, starting):
    starting[...] = layers_backward(received[...].astype(F32), full, (bend_0, bend_1), width_scale).astype(BF16)


def crossed_backward_kernel(width_scale, missing, received, full, bend_0, bend_1, starting):
    last = lax.axis_index("layer") == lax.axis_size("layer") - 1
    cotangent = jnp.where(last, missing[...], received[...].astype(F32))
    starting[...] = layers_backward(cotangent, full, (bend_0, bend_1), width_scale).astype(BF16)


def flip_kernel(input_0, input_1, flipped_0, flipped_1):
    flipped_0[...] = input_0[...].T
    flipped_1[...] = input_1[...].T


def block_of(flipped, signal, at, turns, across, shards):
    rows = flipped.shape[0] // shards
    return times(flipped[rows_of(at, turns, across, rows, shards)], signal[...]).astype(BF16)


def far_gradient_kernel(width_scale, shards, missing, within, crossed, full, flipped_0, flipped_1, bend_0, bend_1,
                        fx, ux, dx, signal_0, signal_1):
    at = lax.axis_index("dp")
    cotangent = turning(missing, within, crossed)
    signal_1[...] = (cotangent * bend_1[...]).astype(BF16)
    cotangent = cotangent + step_size * width_scale * pull_back(signal_1[...], full[1])
    signal_0[...] = (cotangent * bend_0[...]).astype(BF16)
    for layer_at, flipped, signal in ((0, flipped_0, signal_0), (1, flipped_1, signal_1)):
        fx[layer_at] = block_of(flipped, signal, at, 2, True, shards)
        ux[layer_at] = block_of(flipped, signal, at, 1, True, shards)
        dx[layer_at] = block_of(flipped, signal, at, -1, True, shards)


def near_gradient_kernel(shards, flipped_0, flipped_1, signal_0, signal_1, far, ox, u0, u1, d0, d1, own):
    at = lax.axis_index("dp")
    for layer_at, flipped, signal in ((0, flipped_0, signal_0), (1, flipped_1, signal_1)):
        far[layer_at] = block_of(flipped, signal, at, 2, False, shards)
        ox[layer_at] = block_of(flipped, signal, at, 0, True, shards)
        (u0, u1)[layer_at][...] = block_of(flipped, signal, at, 1, False, shards)
        (d0, d1)[layer_at][...] = block_of(flipped, signal, at, -1, False, shards)
        own[layer_at] = block_of(flipped, signal, at, 0, False, shards)


def settle_kernel(kept, within, crossed, missing, within_back, crossed_back, current_in, cotangent_in):
    current_in[...] = entering(kept, within, crossed)
    cotangent_in[...] = turning(missing, within_back, crossed_back)


def sum_of(*values):
    total = values[0].astype(F32)
    for value in values[1:]:
        total = total + value.astype(F32)
    return total


def relay_kernel(far, from_far, relay_0, relay_1):
    relay_0[...] = sum_of(far[0], from_far[0]).astype(BF16)
    relay_1[...] = sum_of(far[1], from_far[1]).astype(BF16)


def across_kernel(ox, before, after, across):
    across[...] = sum_of(ox[...], before[...], after[...]).astype(BF16)


def onward_kernel(u0, relay_0, d1, relay_1, up_1, down_0, own, onward_0, back_1, partial):
    onward_0[...] = sum_of(u0[...], relay_0[...]).astype(BF16)
    back_1[...] = sum_of(d1[...], relay_1[...]).astype(BF16)
    partial[0] = sum_of(own[0], down_0[...])
    partial[1] = sum_of(own[1], up_1[...])


def update_kernel(row_scale, weights, momentum, partial, across, up_0, down_1,
                  new_weights, new_momentum, both, first, second):
    for layer_at in range(2):
        total = sum_of(partial[layer_at], across[layer_at], (up_0, down_1)[layer_at][...])
        moved = momentum_decay * momentum[layer_at] + total * row_scale
        new_momentum[layer_at] = moved
        stepped = weights[layer_at] - learn_rate * moved
        new_weights[layer_at] = stepped
        both[layer_at] = stepped.astype(BF16)
        (first, second)[layer_at][...] = stepped.astype(BF16)


def local(weights, momentum, boundary, adjoint, target):
    shards = lax.axis_size("dp")
    layers, own_rows, width = weights.shape
    rows = boundary.shape[1]
    width_scale = 1.0 / math.sqrt(width)
    row_scale = 1.0 / math.sqrt(rows * shards)
    state = (rows, width)
    shard = (layers, own_rows, width)
    block = (own_rows, width)
    whole = (layers, width, width)
    product = rows * width * width
    own = on_device(round_kernel, [(shard, BF16), (block, BF16), (block, BF16)], (weights,))

    def step(_, held):
        weights, momentum, kept, cotangent, both, first, second = held
        b0 = turned(first, 1)
        a1 = turned(second, -1)
        b1 = turned(second, 1)
        a0 = turned(first, -1)
        other = swapped(both)
        f0 = turned(b0, 1)
        f1 = turned(a1, -1)
        other_before = turned(other, 1)
        other_after = turned(other, -1)
        partly, far = on_device(near_kernel, [(whole, BF16), (shard, BF16)], (both, other, b0, b1, a0, a1, f0, f1))
        full, outgoing = on_device(
            functools.partial(first_forward_kernel, width_scale), [(whole, BF16), (state, BF16)],
            (partly, other_before, other_after, swapped(far), kept), 4 * product, {0: 0},
        )
        crossed = passed(outgoing, 1, True)
        within = passed(outgoing, 1, False)
        from_within = on_device(
            functools.partial(within_forward_kernel, width_scale), [(state, BF16)], (within, full), 4 * product,
        )[0]
        crossed_last = passed(from_within, 1, True)
        from_crossed = on_device(
            functools.partial(crossed_forward_kernel, width_scale), [(state, BF16)], (kept, crossed, full), 4 * product,
        )[0]
        entered = (passed(from_crossed, 1, False), crossed_last)
        missing, input_0, input_1, bend_0, bend_1, starting = on_device(
            functools.partial(turn_kernel, width_scale),
            [(state, F32)] + [(state, BF16)] * 2 + [(state, F32)] * 2 + [(state, BF16)],
            (kept, *entered, full, target, cotangent), 8 * product,
        )
        bends = (bend_0, bend_1)
        crossed = passed(starting, -1, True)
        within = passed(starting, -1, False)
        flipped = on_device(flip_kernel, [((width, rows), BF16)] * 2, (input_0, input_1))
        from_within = on_device(
            functools.partial(within_backward_kernel, width_scale), [(state, BF16)], (within, full, *bends), 4 * product,
        )[0]
        crossed_last = passed(from_within, -1, True)
        from_crossed = on_device(
            functools.partial(crossed_backward_kernel, width_scale), [(state, BF16)],
            (missing, crossed, full, *bends), 4 * product,
        )[0]
        returned = (missing, passed(from_crossed, -1, False), crossed_last)
        fx, ux, dx, *signals = on_device(
            functools.partial(far_gradient_kernel, width_scale, shards),
            [(shard, BF16)] * 3 + [(state, BF16)] * 2, (*returned, full, *flipped, *bends), 4 * product,
        )
        from_far = swapped(fx)
        before = turned(ux, 1)
        after = turned(dx, -1)
        far, ox, u0, u1, d0, d1, mine = on_device(
            functools.partial(near_gradient_kernel, shards),
            [(shard, BF16)] * 2 + [(block, BF16)] * 4 + [(shard, BF16)], (*flipped, *signals), 2 * product,
        )
        up_1 = turned(u1, 1)
        down_0 = turned(d0, -1)
        relay_0, relay_1 = on_device(relay_kernel, [(block, BF16)] * 2, (far, from_far))
        relay_0 = turned(relay_0, 1)
        relay_1 = turned(relay_1, -1)
        across = swapped(on_device(across_kernel, [(shard, BF16)], (ox, before, after))[0])
        onward_0, back_1, partial = on_device(
            onward_kernel, [(block, BF16)] * 2 + [(shard, F32)], (u0, relay_0, d1, relay_1, up_1, down_0, mine),
        )
        current_in, cotangent_in = on_device(settle_kernel, [(state, F32)] * 2, (kept, *entered, *returned))
        weights, momentum, *rounded = on_device(
            functools.partial(update_kernel, row_scale),
            [(shard, F32)] * 2 + [(shard, BF16), (block, BF16), (block, BF16)],
            (weights, momentum, partial, across, turned(onward_0, 1), turned(back_1, -1)),
        )
        return (weights, momentum, current_in, cotangent_in, *rounded)

    held = lax.fori_loop(0, STEPS, step, (weights, momentum, boundary[0], adjoint[0], *own))
    weights, momentum, current_in, cotangent_in = held[:4]
    return (weights, momentum, current_in[None], cotangent_in[None])


def solution(mesh):
    placed = (
        P("layer", "dp", None),
        P("layer", "dp", None),
        P("layer", "dp", None),
        P("layer", "dp", None),
        P("dp", None),
    )
    return jax.shard_map(
        local,
        mesh=mesh,
        in_specs=placed,
        out_specs=(
            P("layer", "dp", None),
            P("layer", "dp", None),
            P("layer", "dp", None),
            P("layer", "dp", None),
        ),
        check_vma=False,
    )
```

```python
import functools
import math

import jax
import jax.numpy as jnp
from jax import lax
from jax.experimental import pallas as pl
from jax.experimental.pallas import tpu as pltpu
from jax.sharding import PartitionSpec as P

STEPS = 2
SWEEPS = 2


step_size = 0.5
momentum_decay = 0.9
learn_rate = 0.05
HALVES = 2
F32 = jnp.float32
BF16 = jnp.bfloat16


def passed(value, by, crossing):
    groups = lax.axis_size("layer")
    pairs = [(i, i + by) for i in range(groups) if 0 <= i + by < groups]
    return lax.ppermute(value, "layer", [(i, j) for i, j in pairs if (i // 2 != j // 2) == crossing])


def turned(value, by):
    shards = lax.axis_size("dp")
    return lax.ppermute(value, "dp", [(i, (i + HALVES * by) % shards) for i in range(shards)])


def swapped(value):
    shards = lax.axis_size("dp")
    return lax.ppermute(value, "dp", [(i, i ^ 1) for i in range(shards)])


def on_device(body, outs, operands, flops=0, in_place=None, held=()):
    whole = pl.BlockSpec(memory_space=pltpu.VMEM)
    shapes = [jax.ShapeDtypeStruct(shape, kind) for shape, kind in outs]
    moved = sum(math.prod(o.shape) * o.dtype.itemsize for o in [*operands, *shapes])
    return pl.pallas_call(
        body,
        out_shape=shapes,
        in_specs=[whole] * len(operands),
        out_specs=[whole] * len(shapes),
        input_output_aliases=in_place or {},
        scratch_shapes=[pltpu.VMEM(shape, kind) for shape, kind in held],
        cost_estimate=pl.CostEstimate(flops=flops, bytes_accessed=moved, transcendentals=0),
        compiler_params=pltpu.CompilerParams(vmem_limit_bytes=20 * 2**20),
    )(*operands)


def rows_of(at, turns, across, rows, shards):
    place = lax.rem(at + HALVES * turns + shards, shards)
    if across:
        place = place + 1 - 2 * lax.rem(place, 2)
    return pl.ds(pl.multiple_of(place * rows, rows), rows)


def times(left, right):
    return jnp.dot(left, right, preferred_element_type=F32)


def pull_back(signal, matrix):
    return lax.dot_general(signal, matrix, (((1,), (1,)), ((), ())), preferred_element_type=F32)


def round_kernel(weights, both, first, second):
    rounded = weights[...].astype(BF16)
    both[...] = rounded
    first[...] = rounded[0]
    second[...] = rounded[1]


def layers_forward(current, full, width_scale, inputs=None, bends=None):
    def layer(layer_at, carry):
        rounded = current[...].astype(BF16)
        squashed = jnp.tanh(times(rounded, full[layer_at]) * width_scale)
        current[...] = current[...] + step_size * squashed
        if inputs is not None:
            inputs[layer_at] = rounded
            bends[layer_at] = 1.0 - squashed * squashed
        return carry

    lax.fori_loop(0, full.shape[0], layer, 0)


def layers_backward(cotangent, full, bends, width_scale):
    def layer(done, carry):
        layer_at = full.shape[0] - 1 - done
        signal = (cotangent[...] * bends[layer_at]).astype(BF16)
        cotangent[...] = cotangent[...] + step_size * width_scale * pull_back(signal, full[layer_at])
        return carry

    lax.fori_loop(0, full.shape[0], layer, 0)


def entering(kept, within, crossed):
    at = lax.axis_index("layer")
    arrived = jnp.where(lax.rem(at, 2) == 1, within[...], crossed[...])
    return jnp.where(at == 0, kept[...], arrived.astype(F32))


def turning(missing, within, crossed):
    at = lax.axis_index("layer")
    arrived = jnp.where(lax.rem(at, 2) == 0, within[...], crossed[...])
    return jnp.where(at == lax.axis_size("layer") - 1, missing[...], arrived.astype(F32))


def near_kernel(fresh, *refs):
    own, other, b0, b1, a0, a1, f0, f1, kept, *refs = refs
    full, far, current = refs[-3:]
    at = lax.axis_index("dp")
    shards = lax.axis_size("dp")
    rows = own.shape[1]
    for layer_at in range(2):
        def put(piece, turns, across):
            full[layer_at, rows_of(at, turns, across, rows, shards)] = piece

        put(own[layer_at], 0, False)
        put(other[layer_at], 0, True)
        put((b0, b1)[layer_at][...], -1, False)
        put((a0, a1)[layer_at][...], 1, False)
        piece = (f0, f1)[layer_at][...]
        put(piece, 2, False)
        far[layer_at] = piece
    current[...] = kept[...] if fresh else entering(kept, *refs[:2])


def first_forward_kernel(width_scale, partly, before, after, far, entered, full, outgoing, current):
    at = lax.axis_index("dp")
    shards = lax.axis_size("dp")
    rows = far.shape[1]
    for layer_at in range(2):
        for piece, turns in ((before, -1), (after, 1), (far, 2)):
            full[layer_at, rows_of(at, turns, True, rows, shards)] = piece[layer_at]
    current[...] = entered[...]
    layers_forward(current, full, width_scale)
    outgoing[...] = current[...].astype(BF16)


def within_forward_kernel(width_scale, received, full, outgoing, current):
    current[...] = received[...].astype(F32)
    layers_forward(current, full, width_scale)
    outgoing[...] = current[...].astype(BF16)


def crossed_forward_kernel(width_scale, kept, received, full, outgoing, current):
    current[...] = jnp.where(lax.axis_index("layer") == 0, kept[...], received[...].astype(F32))
    layers_forward(current, full, width_scale)
    outgoing[...] = current[...].astype(BF16)


def turn_kernel(width_scale, fresh, kept, within, crossed, full, target, *refs):
    missing, inputs, bends, starting, current = refs[-5:]
    current[...] = entering(kept, within, crossed)
    layers_forward(current, full, width_scale, inputs, bends)
    missing[...] = current[...] - target[...]
    current[...] = refs[0][...] if fresh else turning(*refs[:3])
    layers_backward(current, full, bends, width_scale)
    starting[...] = current[...].astype(BF16)


def within_backward_kernel(width_scale, received, full, bends, starting, cotangent):
    cotangent[...] = received[...].astype(F32)
    layers_backward(cotangent, full, bends, width_scale)
    starting[...] = cotangent[...].astype(BF16)


def crossed_backward_kernel(width_scale, missing, received, full, bends, starting, cotangent):
    last = lax.axis_index("layer") == lax.axis_size("layer") - 1
    cotangent[...] = jnp.where(last, missing[...], received[...].astype(F32))
    layers_backward(cotangent, full, bends, width_scale)
    starting[...] = cotangent[...].astype(BF16)


def flip_kernel(inputs, flipped):
    def layer(layer_at, carry):
        flipped[layer_at] = inputs[layer_at].T
        return carry

    lax.fori_loop(0, inputs.shape[0], layer, 0)


def block_of(flipped, signals, layer_at, at, turns, across, shards):
    rows = flipped.shape[1] // shards
    return times(flipped[layer_at, rows_of(at, turns, across, rows, shards)], signals[layer_at]).astype(BF16)


def far_gradient_kernel(width_scale, shards, missing, within, crossed, full, flipped, bends, fx, ux, dx, signals):
    at = lax.axis_index("dp")
    cotangent = turning(missing, within, crossed)
    signals[1] = (cotangent * bends[1]).astype(BF16)
    cotangent = cotangent + step_size * width_scale * pull_back(signals[1], full[1])
    signals[0] = (cotangent * bends[0]).astype(BF16)

    def layer(layer_at, carry):
        fx[layer_at] = block_of(flipped, signals, layer_at, at, 2, True, shards)
        ux[layer_at] = block_of(flipped, signals, layer_at, at, 1, True, shards)
        dx[layer_at] = block_of(flipped, signals, layer_at, at, -1, True, shards)
        return carry

    lax.fori_loop(0, fx.shape[0], layer, 0)


def near_gradient_kernel(shards, flipped, signals, far, ox, u0, u1, d0, d1, own):
    at = lax.axis_index("dp")

    def layer(layer_at, carry):
        far[layer_at] = block_of(flipped, signals, layer_at, at, 2, False, shards)
        ox[layer_at] = block_of(flipped, signals, layer_at, at, 0, True, shards)
        own[layer_at] = block_of(flipped, signals, layer_at, at, 0, False, shards)
        return carry

    lax.fori_loop(0, far.shape[0], layer, 0)
    for layer_at in range(2):
        (u0, u1)[layer_at][...] = block_of(flipped, signals, layer_at, at, 1, False, shards)
        (d0, d1)[layer_at][...] = block_of(flipped, signals, layer_at, at, -1, False, shards)


def settle_kernel(kept, within, crossed, missing, within_back, crossed_back, current_in, cotangent_in):
    current_in[...] = entering(kept, within, crossed)
    cotangent_in[...] = turning(missing, within_back, crossed_back)


def sum_of(*values):
    total = values[0].astype(F32)
    for value in values[1:]:
        total = total + value.astype(F32)
    return total


def relay_kernel(far, from_far, relay_0, relay_1):
    relay_0[...] = sum_of(far[0], from_far[0]).astype(BF16)
    relay_1[...] = sum_of(far[1], from_far[1]).astype(BF16)


def across_kernel(ox, before, after, across):
    across[...] = sum_of(ox[...], before[...], after[...]).astype(BF16)


def onward_kernel(u0, relay_0, d1, relay_1, up_1, down_0, own, onward_0, back_1, partial):
    onward_0[...] = sum_of(u0[...], relay_0[...]).astype(BF16)
    back_1[...] = sum_of(d1[...], relay_1[...]).astype(BF16)
    partial[0] = sum_of(own[0], down_0[...])
    partial[1] = sum_of(own[1], up_1[...])


def update_kernel(row_scale, weights, momentum, partial, across, up_0, down_1, new_weights, new_momentum, *rounded):
    for layer_at in range(2):
        total = sum_of(partial[layer_at], across[layer_at], (up_0, down_1)[layer_at][...])
        moved = momentum_decay * momentum[layer_at] + total * row_scale
        new_momentum[layer_at] = moved
        stepped = weights[layer_at] - learn_rate * moved
        new_weights[layer_at] = stepped
        if rounded:
            rounded[0][layer_at] = stepped.astype(BF16)
            rounded[1 + layer_at][...] = stepped.astype(BF16)


def local(weights, momentum, boundary, adjoint, target):
    shards = lax.axis_size("dp")
    layers, own_rows, width = weights.shape
    rows = boundary.shape[1]
    width_scale = 1.0 / math.sqrt(width)
    row_scale = 1.0 / math.sqrt(rows * shards)
    state = (rows, width)
    shard = (layers, own_rows, width)
    block = (own_rows, width)
    whole = (layers, width, width)
    product = rows * width * width
    work = [(state, F32)]
    kept = boundary[0]
    entered = ()
    returned = (adjoint[0],)
    own = on_device(round_kernel, [(shard, BF16), (block, BF16), (block, BF16)], (weights,))
    for update_at in range(STEPS):
        fresh = update_at == 0
        both, first, second = own
        b0 = turned(first, 1)
        a1 = turned(second, -1)
        b1 = turned(second, 1)
        a0 = turned(first, -1)
        other = swapped(both)
        f0 = turned(b0, 1)
        f1 = turned(a1, -1)
        other_before = turned(other, 1)
        other_after = turned(other, -1)
        partly, far, current = on_device(
            functools.partial(near_kernel, fresh), [(whole, BF16), (shard, BF16), (state, F32)],
            (both, other, b0, b1, a0, a1, f0, f1, kept, *entered),
        )
        full, outgoing = on_device(
            functools.partial(first_forward_kernel, width_scale), [(whole, BF16), (state, BF16)],
            (partly, other_before, other_after, swapped(far), current), 4 * product, {0: 0}, work,
        )
        crossed = passed(outgoing, 1, True)
        within = passed(outgoing, 1, False)
        from_within = on_device(
            functools.partial(within_forward_kernel, width_scale), [(state, BF16)], (within, full), 4 * product, held=work,
        )[0]
        crossed_last = passed(from_within, 1, True)
        from_crossed = on_device(
            functools.partial(crossed_forward_kernel, width_scale), [(state, BF16)], (kept, crossed, full), 4 * product,
            held=work,
        )[0]
        entered = (passed(from_crossed, 1, False), crossed_last)
        missing, inputs, bends, starting = on_device(
            functools.partial(turn_kernel, width_scale, fresh),
            [(state, F32), ((layers, *state), BF16), ((layers, *state), F32), (state, BF16)],
            (kept, *entered, full, target, *returned), 8 * product, held=work,
        )
        crossed = passed(starting, -1, True)
        within = passed(starting, -1, False)
        flipped = on_device(flip_kernel, [((layers, width, rows), BF16)], (inputs,))[0]
        from_within = on_device(
            functools.partial(within_backward_kernel, width_scale), [(state, BF16)], (within, full, bends), 4 * product,
            held=work,
        )[0]
        crossed_last = passed(from_within, -1, True)
        from_crossed = on_device(
            functools.partial(crossed_backward_kernel, width_scale), [(state, BF16)],
            (missing, crossed, full, bends), 4 * product, held=work,
        )[0]
        returned = (missing, passed(from_crossed, -1, False), crossed_last)
        fx, ux, dx, signals = on_device(
            functools.partial(far_gradient_kernel, width_scale, shards),
            [(shard, BF16)] * 3 + [((layers, *state), BF16)], (*returned, full, flipped, bends), 4 * product,
        )
        from_far = swapped(fx)
        before = turned(ux, 1)
        after = turned(dx, -1)
        far, ox, u0, u1, d0, d1, mine = on_device(
            functools.partial(near_gradient_kernel, shards),
            [(shard, BF16)] * 2 + [(block, BF16)] * 4 + [(shard, BF16)], (flipped, signals), 2 * product,
        )
        up_1 = turned(u1, 1)
        down_0 = turned(d0, -1)
        relay_0, relay_1 = on_device(relay_kernel, [(block, BF16)] * 2, (far, from_far))
        relay_0 = turned(relay_0, 1)
        relay_1 = turned(relay_1, -1)
        across = swapped(on_device(across_kernel, [(shard, BF16)], (ox, before, after))[0])
        onward_0, back_1, partial = on_device(
            onward_kernel, [(block, BF16)] * 2 + [(shard, F32)], (u0, relay_0, d1, relay_1, up_1, down_0, mine),
        )
        rounded = [] if update_at == STEPS - 1 else [(shard, BF16), (block, BF16), (block, BF16)]
        weights, momentum, *own = on_device(
            functools.partial(update_kernel, row_scale), [(shard, F32), (shard, F32), *rounded],
            (weights, momentum, partial, across, turned(onward_0, 1), turned(back_1, -1)),
        )
    current_in, cotangent_in = on_device(settle_kernel, [(state, F32)] * 2, (kept, *entered, *returned))
    return (weights, momentum, current_in[None], cotangent_in[None])


def solution(mesh):
    placed = (
        P("layer", "dp", None),
        P("layer", "dp", None),
        P("layer", "dp", None),
        P("layer", "dp", None),
        P("dp", None),
    )
    return jax.shard_map(
        local,
        mesh=mesh,
        in_specs=placed,
        out_specs=(
            P("layer", "dp", None),
            P("layer", "dp", None),
            P("layer", "dp", None),
            P("layer", "dp", None),
        ),
        check_vma=False,
    )
```

```python
import functools
import math

import jax
import jax.numpy as jnp
from jax import lax
from jax.experimental import pallas as pl
from jax.experimental.pallas import tpu as pltpu
from jax.sharding import PartitionSpec as P

STEPS = 2
SWEEPS = 2


step_size = 0.5
momentum_decay = 0.9
learn_rate = 0.05
HALVES = 2
F32 = jnp.float32
BF16 = jnp.bfloat16


def passed(value, by, crossing):
    groups = lax.axis_size("layer")
    pairs = [(i, i + by) for i in range(groups) if 0 <= i + by < groups]
    return lax.ppermute(value, "layer", [(i, j) for i, j in pairs if (i // 2 != j // 2) == crossing])


def turned(value, by):
    shards = lax.axis_size("dp")
    return lax.ppermute(value, "dp", [(i, (i + HALVES * by) % shards) for i in range(shards)])


def swapped(value):
    shards = lax.axis_size("dp")
    return lax.ppermute(value, "dp", [(i, i ^ 1) for i in range(shards)])


def on_device(body, outs, operands, flops=0, in_place=None):
    whole = pl.BlockSpec(memory_space=pltpu.VMEM)
    shapes = [jax.ShapeDtypeStruct(shape, kind) for shape, kind in outs]
    moved = sum(math.prod(o.shape) * o.dtype.itemsize for o in [*operands, *shapes])
    return pl.pallas_call(
        body,
        out_shape=shapes,
        in_specs=[whole] * len(operands),
        out_specs=[whole] * len(shapes),
        input_output_aliases=in_place or {},
        cost_estimate=pl.CostEstimate(flops=flops, bytes_accessed=moved, transcendentals=0),
        compiler_params=pltpu.CompilerParams(vmem_limit_bytes=20 * 2**20),
    )(*operands)


def rows_of(at, turns, across, rows, shards):
    place = lax.rem(at + HALVES * turns + shards, shards)
    if across:
        place = place + 1 - 2 * lax.rem(place, 2)
    return pl.ds(pl.multiple_of(place * rows, rows), rows)


def times(left, right):
    return jnp.dot(left, right, preferred_element_type=F32)


def pull_back(signal, matrix):
    return lax.dot_general(signal, matrix, (((1,), (1,)), ((), ())), preferred_element_type=F32)


def round_kernel(weights, both, first, second):
    rounded = weights[...].astype(BF16)
    both[...] = rounded
    first[...] = rounded[0]
    second[...] = rounded[1]


def layers_forward(current, full, width_scale, inputs=(), bends=()):
    for layer_at in range(full.shape[0]):
        rounded = current.astype(BF16)
        squashed = jnp.tanh(times(rounded, full[layer_at]) * width_scale)
        current = current + step_size * squashed
        if inputs:
            inputs[layer_at][...] = rounded
            bends[layer_at][...] = 1.0 - squashed * squashed
    return current


def layers_backward(cotangent, full, bends, width_scale):
    for layer_at in reversed(range(full.shape[0])):
        signal = (cotangent * bends[layer_at][...]).astype(BF16)
        cotangent = cotangent + step_size * width_scale * pull_back(signal, full[layer_at])
    return cotangent


def entering(kept, within, crossed):
    at = lax.axis_index("layer")
    arrived = jnp.where(lax.rem(at, 2) == 1, within[...], crossed[...])
    return jnp.where(at == 0, kept[...], arrived.astype(F32))


def turning(missing, within, crossed):
    at = lax.axis_index("layer")
    arrived = jnp.where(lax.rem(at, 2) == 0, within[...], crossed[...])
    return jnp.where(at == lax.axis_size("layer") - 1, missing[...], arrived.astype(F32))


def near_kernel(fresh, *refs):
    own, other, b0, b1, a0, a1, f0, f1, kept, *refs = refs
    full, far, current = refs[-3:]
    at = lax.axis_index("dp")
    shards = lax.axis_size("dp")
    rows = own.shape[1]
    for layer_at in range(2):
        def put(piece, turns, across):
            full[layer_at, rows_of(at, turns, across, rows, shards)] = piece

        put(own[layer_at], 0, False)
        put(other[layer_at], 0, True)
        put((b0, b1)[layer_at][...], -1, False)
        put((a0, a1)[layer_at][...], 1, False)
        piece = (f0, f1)[layer_at][...]
        put(piece, 2, False)
        far[layer_at] = piece
    current[...] = kept[...] if fresh else entering(kept, *refs[:2])


def first_forward_kernel(width_scale, partly, before, after, far, current, full, outgoing):
    at = lax.axis_index("dp")
    shards = lax.axis_size("dp")
    rows = far.shape[1]
    for layer_at in range(2):
        for piece, turns in ((before, -1), (after, 1), (far, 2)):
            full[layer_at, rows_of(at, turns, True, rows, shards)] = piece[layer_at]
    outgoing[...] = layers_forward(current[...], full, width_scale).astype(BF16)


def within_forward_kernel(width_scale, received, full, outgoing):
    outgoing[...] = layers_forward(received[...].astype(F32), full, width_scale).astype(BF16)


def crossed_forward_kernel(width_scale, kept, received, full, outgoing):
    current = jnp.where(lax.axis_index("layer") == 0, kept[...], received[...].astype(F32))
    outgoing[...] = layers_forward(current, full, width_scale).astype(BF16)


def turn_kernel(width_scale, fresh, kept, within, crossed, full, target, *refs):
    if fresh:
        adjoint, *refs = refs
        cotangent = adjoint[...]
    else:
        ending, within_back, crossed_back, *refs = refs
        cotangent = turning(ending, within_back, crossed_back)
    missing, input_0, input_1, bend_0, bend_1, starting = refs
    bends = (bend_0, bend_1)
    finals = layers_forward(entering(kept, within, crossed), full, width_scale, (input_0, input_1), bends)
    missing[...] = finals - target[...]
    starting[...] = layers_backward(cotangent, full, bends, width_scale).astype(BF16)


def within_backward_kernel(width_scale, received, full, bend_0, bend_1, starting):
    starting[...] = layers_backward(received[...].astype(F32), full, (bend_0, bend_1), width_scale).astype(BF16)


def crossed_backward_kernel(width_scale, missing, received, full, bend_0, bend_1, starting):
    last = lax.axis_index("layer") == lax.axis_size("layer") - 1
    cotangent = jnp.where(last, missing[...], received[...].astype(F32))
    starting[...] = layers_backward(cotangent, full, (bend_0, bend_1), width_scale).astype(BF16)


def flip_kernel(input_0, input_1, flipped_0, flipped_1):
    flipped_0[...] = input_0[...].T
    flipped_1[...] = input_1[...].T


def block_of(flipped, signal, at, turns, across, shards):
    rows = flipped.shape[0] // shards
    return times(flipped[rows_of(at, turns, across, rows, shards)], signal[...]).astype(BF16)


def far_gradient_kernel(width_scale, shards, missing, within, crossed, full, flipped_0, flipped_1, bend_0, bend_1,
                        fx, ux, dx, signal_0, signal_1):
    at = lax.axis_index("dp")
    cotangent = turning(missing, within, crossed)
    signal_1[...] = (cotangent * bend_1[...]).astype(BF16)
    cotangent = cotangent + step_size * width_scale * pull_back(signal_1[...], full[1])
    signal_0[...] = (cotangent * bend_0[...]).astype(BF16)
    for layer_at, flipped, signal in ((0, flipped_0, signal_0), (1, flipped_1, signal_1)):
        fx[layer_at] = block_of(flipped, signal, at, 2, True, shards)
        ux[layer_at] = block_of(flipped, signal, at, 1, True, shards)
        dx[layer_at] = block_of(flipped, signal, at, -1, True, shards)


def near_gradient_kernel(shards, flipped_0, flipped_1, signal_0, signal_1, far, ox, u0, d1, own):
    at = lax.axis_index("dp")
    for layer_at, flipped, signal in ((0, flipped_0, signal_0), (1, flipped_1, signal_1)):
        far[layer_at] = block_of(flipped, signal, at, 2, False, shards)
        ox[layer_at] = block_of(flipped, signal, at, 0, True, shards)
        own[layer_at] = block_of(flipped, signal, at, 0, False, shards)
    u0[...] = block_of(flipped_0, signal_0, at, 1, False, shards)
    d1[...] = block_of(flipped_1, signal_1, at, -1, False, shards)


def settle_kernel(kept, within, crossed, missing, within_back, crossed_back, current_in, cotangent_in):
    current_in[...] = entering(kept, within, crossed)
    cotangent_in[...] = turning(missing, within_back, crossed_back)


def sum_of(*values):
    total = values[0].astype(F32)
    for value in values[1:]:
        total = total + value.astype(F32)
    return total


def relay_kernel(far, from_far, relay_0, relay_1):
    relay_0[...] = sum_of(far[0], from_far[0]).astype(BF16)
    relay_1[...] = sum_of(far[1], from_far[1]).astype(BF16)


def across_kernel(shards, ox, before, after, flipped_0, flipped_1, signal_0, signal_1, across, d0, u1):
    at = lax.axis_index("dp")
    across[...] = sum_of(ox[...], before[...], after[...]).astype(BF16)
    d0[...] = block_of(flipped_0, signal_0, at, -1, False, shards)
    u1[...] = block_of(flipped_1, signal_1, at, 1, False, shards)


def onward_kernel(u0, relay_0, d1, relay_1, onward_0, back_1):
    onward_0[...] = sum_of(u0[...], relay_0[...]).astype(BF16)
    back_1[...] = sum_of(d1[...], relay_1[...]).astype(BF16)


def update_kernel(row_scale, weights, momentum, own, across, up_0, up_1, down_0, down_1,
                  new_weights, new_momentum, *rounded):
    for layer_at in range(2):
        total = sum_of(own[layer_at], across[layer_at], (up_0, up_1)[layer_at][...], (down_0, down_1)[layer_at][...])
        moved = momentum_decay * momentum[layer_at] + total * row_scale
        new_momentum[layer_at] = moved
        stepped = weights[layer_at] - learn_rate * moved
        new_weights[layer_at] = stepped
        if rounded:
            rounded[0][layer_at] = stepped.astype(BF16)
            rounded[1 + layer_at][...] = stepped.astype(BF16)


def local(weights, momentum, boundary, adjoint, target):
    shards = lax.axis_size("dp")
    layers, own_rows, width = weights.shape
    rows = boundary.shape[1]
    width_scale = 1.0 / math.sqrt(width)
    row_scale = 1.0 / math.sqrt(rows * shards)
    state = (rows, width)
    shard = (layers, own_rows, width)
    block = (own_rows, width)
    whole = (layers, width, width)
    product = rows * width * width
    kept = boundary[0]
    entered = ()
    returned = (adjoint[0],)
    own = on_device(round_kernel, [(shard, BF16), (block, BF16), (block, BF16)], (weights,))
    for update_at in range(STEPS):
        fresh = update_at == 0
        both, first, second = own
        b0 = turned(first, 1)
        a1 = turned(second, -1)
        b1 = turned(second, 1)
        a0 = turned(first, -1)
        other = swapped(both)
        f0 = turned(b0, 1)
        f1 = turned(a1, -1)
        other_before = turned(other, 1)
        other_after = turned(other, -1)
        partly, far, current = on_device(
            functools.partial(near_kernel, fresh), [(whole, BF16), (shard, BF16), (state, F32)],
            (both, other, b0, b1, a0, a1, f0, f1, kept, *entered),
        )
        full, outgoing = on_device(
            functools.partial(first_forward_kernel, width_scale), [(whole, BF16), (state, BF16)],
            (partly, other_before, other_after, swapped(far), current), 4 * product, {0: 0},
        )
        within = passed(outgoing, 1, False)
        crossed = passed(outgoing, 1, True)
        from_within = on_device(
            functools.partial(within_forward_kernel, width_scale), [(state, BF16)], (within, full), 4 * product,
        )[0]
        crossed_last = passed(from_within, 1, True)
        from_crossed = on_device(
            functools.partial(crossed_forward_kernel, width_scale), [(state, BF16)], (kept, crossed, full), 4 * product,
        )[0]
        entered = (passed(from_crossed, 1, False), crossed_last)
        missing, input_0, input_1, bend_0, bend_1, starting = on_device(
            functools.partial(turn_kernel, width_scale, fresh),
            [(state, F32)] + [(state, BF16)] * 2 + [(state, F32)] * 2 + [(state, BF16)],
            (kept, *entered, full, target, *returned), 8 * product,
        )
        bends = (bend_0, bend_1)
        within = passed(starting, -1, False)
        crossed = passed(starting, -1, True)
        flipped = on_device(flip_kernel, [((width, rows), BF16)] * 2, (input_0, input_1))
        from_within = on_device(
            functools.partial(within_backward_kernel, width_scale), [(state, BF16)], (within, full, *bends), 4 * product,
        )[0]
        crossed_last = passed(from_within, -1, True)
        from_crossed = on_device(
            functools.partial(crossed_backward_kernel, width_scale), [(state, BF16)],
            (missing, crossed, full, *bends), 4 * product,
        )[0]
        returned = (missing, passed(from_crossed, -1, False), crossed_last)
        fx, ux, dx, *signals = on_device(
            functools.partial(far_gradient_kernel, width_scale, shards),
            [(shard, BF16)] * 3 + [(state, BF16)] * 2, (*returned, full, *flipped, *bends), 4 * product,
        )
        from_far = swapped(fx)
        before = turned(ux, 1)
        after = turned(dx, -1)
        far, ox, u0, d1, mine = on_device(
            functools.partial(near_gradient_kernel, shards),
            [(shard, BF16)] * 2 + [(block, BF16)] * 2 + [(shard, BF16)], (*flipped, *signals), 2 * product,
        )
        relay_0, relay_1 = on_device(relay_kernel, [(block, BF16)] * 2, (far, from_far))
        relay_0 = turned(relay_0, 1)
        relay_1 = turned(relay_1, -1)
        across, d0, u1 = on_device(
            functools.partial(across_kernel, shards), [(shard, BF16), (block, BF16), (block, BF16)],
            (ox, before, after, *flipped, *signals), product,
        )
        across = swapped(across)
        up_1 = turned(u1, 1)
        down_0 = turned(d0, -1)
        onward_0, back_1 = on_device(onward_kernel, [(block, BF16)] * 2, (u0, relay_0, d1, relay_1))
        rounded = [] if update_at == STEPS - 1 else [(shard, BF16), (block, BF16), (block, BF16)]
        weights, momentum, *own = on_device(
            functools.partial(update_kernel, row_scale), [(shard, F32), (shard, F32), *rounded],
            (weights, momentum, mine, across, turned(onward_0, 1), up_1, down_0, turned(back_1, -1)),
        )
    current_in, cotangent_in = on_device(settle_kernel, [(state, F32)] * 2, (kept, *entered, *returned))
    return (weights, momentum, current_in[None], cotangent_in[None])


def solution(mesh):
    placed = (
        P("layer", "dp", None),
        P("layer", "dp", None),
        P("layer", "dp", None),
        P("layer", "dp", None),
        P("dp", None),
    )
    return jax.shard_map(
        local,
        mesh=mesh,
        in_specs=placed,
        out_specs=(
            P("layer", "dp", None),
            P("layer", "dp", None),
            P("layer", "dp", None),
            P("layer", "dp", None),
        ),
        check_vma=False,
    )
```

```python
import functools
import math

import jax
import jax.numpy as jnp
from jax import lax
from jax.experimental import pallas as pl
from jax.experimental.pallas import tpu as pltpu
from jax.sharding import PartitionSpec as P

STEPS = 2
SWEEPS = 2


step_size = 0.5
momentum_decay = 0.9
learn_rate = 0.05
HALVES = 2
F32 = jnp.float32
BF16 = jnp.bfloat16


def passed(value, by, crossing):
    groups = lax.axis_size("layer")
    pairs = [(i, i + by) for i in range(groups) if 0 <= i + by < groups]
    return lax.ppermute(value, "layer", [(i, j) for i, j in pairs if (i // 2 != j // 2) == crossing])


def turned(value, by):
    shards = lax.axis_size("dp")
    return lax.ppermute(value, "dp", [(i, (i + HALVES * by) % shards) for i in range(shards)])


def swapped(value):
    shards = lax.axis_size("dp")
    return lax.ppermute(value, "dp", [(i, i ^ 1) for i in range(shards)])


def on_device(body, outs, operands, flops=0, in_place=None):
    whole = pl.BlockSpec(memory_space=pltpu.VMEM)
    shapes = [jax.ShapeDtypeStruct(shape, kind) for shape, kind in outs]
    moved = sum(math.prod(o.shape) * o.dtype.itemsize for o in [*operands, *shapes])
    return pl.pallas_call(
        body,
        out_shape=shapes,
        in_specs=[whole] * len(operands),
        out_specs=[whole] * len(shapes),
        input_output_aliases=in_place or {},
        cost_estimate=pl.CostEstimate(flops=flops, bytes_accessed=moved, transcendentals=0),
        compiler_params=pltpu.CompilerParams(vmem_limit_bytes=20 * 2**20),
    )(*operands)


def rows_of(at, turns, across, rows, shards):
    place = lax.rem(at + HALVES * turns + shards, shards)
    if across:
        place = place + 1 - 2 * lax.rem(place, 2)
    return pl.ds(pl.multiple_of(place * rows, rows), rows)


def times(left, right):
    return jnp.dot(left, right, preferred_element_type=F32)


def pull_back(signal, matrix):
    return lax.dot_general(signal, matrix, (((1,), (1,)), ((), ())), preferred_element_type=F32)


def round_kernel(weights, both, first, second):
    rounded = weights[...].astype(BF16)
    both[...] = rounded
    first[...] = rounded[0]
    second[...] = rounded[1]


def layers_forward(current, full, width_scale, inputs=(), bends=()):
    for layer_at in range(full.shape[0]):
        rounded = current.astype(BF16)
        squashed = jnp.tanh(times(rounded, full[layer_at]) * width_scale)
        current = current + step_size * squashed
        if inputs:
            inputs[layer_at][...] = rounded
            bends[layer_at][...] = 1.0 - squashed * squashed
    return current


def layers_backward(cotangent, full, bends, width_scale):
    for layer_at in reversed(range(full.shape[0])):
        signal = (cotangent * bends[layer_at][...]).astype(BF16)
        cotangent = cotangent + step_size * width_scale * pull_back(signal, full[layer_at])
    return cotangent


def entering(kept, within, crossed):
    at = lax.axis_index("layer")
    arrived = jnp.where(lax.rem(at, 2) == 1, within[...], crossed[...])
    return jnp.where(at == 0, kept[...], arrived.astype(F32))


def turning(missing, within, crossed):
    at = lax.axis_index("layer")
    arrived = jnp.where(lax.rem(at, 2) == 0, within[...], crossed[...])
    return jnp.where(at == lax.axis_size("layer") - 1, missing[...], arrived.astype(F32))


def near_kernel(own, other, b0, b1, a0, a1, f0, f1, full, far):
    at = lax.axis_index("dp")
    shards = lax.axis_size("dp")
    rows = own.shape[1]
    for layer_at in range(2):
        def put(piece, turns, across):
            full[layer_at, rows_of(at, turns, across, rows, shards)] = piece

        put(own[layer_at], 0, False)
        put(other[layer_at], 0, True)
        put((b0, b1)[layer_at][...], -1, False)
        put((a0, a1)[layer_at][...], 1, False)
        piece = (f0, f1)[layer_at][...]
        put(piece, 2, False)
        far[layer_at] = piece


def across_pieces_kernel(fresh, partly, before, after, kept, *refs):
    full, current = refs[-2:]
    at = lax.axis_index("dp")
    shards = lax.axis_size("dp")
    rows = before.shape[1]
    for layer_at in range(2):
        for piece, turns in ((before, -1), (after, 1)):
            full[layer_at, rows_of(at, turns, True, rows, shards)] = piece[layer_at]
    current[...] = kept[...] if fresh else entering(kept, *refs[:2])


def first_forward_kernel(width_scale, partly, far, current, full, outgoing):
    at = lax.axis_index("dp")
    rows = far.shape[1]
    for layer_at in range(2):
        full[layer_at, rows_of(at, 2, True, rows, lax.axis_size("dp"))] = far[layer_at]
    outgoing[...] = layers_forward(current[...], full, width_scale).astype(BF16)


def within_forward_kernel(width_scale, received, full, outgoing):
    outgoing[...] = layers_forward(received[...].astype(F32), full, width_scale).astype(BF16)


def crossed_forward_kernel(width_scale, kept, received, full, outgoing):
    current = jnp.where(lax.axis_index("layer") == 0, kept[...], received[...].astype(F32))
    outgoing[...] = layers_forward(current, full, width_scale).astype(BF16)


def turn_kernel(width_scale, fresh, kept, within, crossed, full, target, *refs):
    if fresh:
        adjoint, *refs = refs
        cotangent = adjoint[...]
    else:
        ending, within_back, crossed_back, *refs = refs
        cotangent = turning(ending, within_back, crossed_back)
    missing, input_0, input_1, bend_0, bend_1, starting = refs
    bends = (bend_0, bend_1)
    finals = layers_forward(entering(kept, within, crossed), full, width_scale, (input_0, input_1), bends)
    missing[...] = finals - target[...]
    starting[...] = layers_backward(cotangent, full, bends, width_scale).astype(BF16)


def within_backward_kernel(width_scale, received, full, bend_0, bend_1, starting):
    starting[...] = layers_backward(received[...].astype(F32), full, (bend_0, bend_1), width_scale).astype(BF16)


def crossed_backward_kernel(width_scale, missing, received, full, bend_0, bend_1, starting):
    last = lax.axis_index("layer") == lax.axis_size("layer") - 1
    cotangent = jnp.where(last, missing[...], received[...].astype(F32))
    starting[...] = layers_backward(cotangent, full, (bend_0, bend_1), width_scale).astype(BF16)


def flip_kernel(input_0, input_1, flipped_0, flipped_1):
    flipped_0[...] = input_0[...].T
    flipped_1[...] = input_1[...].T


def block_of(flipped, signal, at, turns, across, shards):
    rows = flipped.shape[0] // shards
    return times(flipped[rows_of(at, turns, across, rows, shards)], signal[...]).astype(BF16)


def far_gradient_kernel(width_scale, shards, missing, within, crossed, full, flipped_0, flipped_1, bend_0, bend_1,
                        fx, ux, dx, signal_0, signal_1):
    at = lax.axis_index("dp")
    cotangent = turning(missing, within, crossed)
    signal_1[...] = (cotangent * bend_1[...]).astype(BF16)
    cotangent = cotangent + step_size * width_scale * pull_back(signal_1[...], full[1])
    signal_0[...] = (cotangent * bend_0[...]).astype(BF16)
    for layer_at, flipped, signal in ((0, flipped_0, signal_0), (1, flipped_1, signal_1)):
        fx[layer_at] = block_of(flipped, signal, at, 2, True, shards)
        ux[layer_at] = block_of(flipped, signal, at, 1, True, shards)
        dx[layer_at] = block_of(flipped, signal, at, -1, True, shards)


def near_gradient_kernel(shards, flipped_0, flipped_1, signal_0, signal_1, far, ox, u0, d1, own):
    at = lax.axis_index("dp")
    for layer_at, flipped, signal in ((0, flipped_0, signal_0), (1, flipped_1, signal_1)):
        far[layer_at] = block_of(flipped, signal, at, 2, False, shards)
        ox[layer_at] = block_of(flipped, signal, at, 0, True, shards)
        own[layer_at] = block_of(flipped, signal, at, 0, False, shards)
    u0[...] = block_of(flipped_0, signal_0, at, 1, False, shards)
    d1[...] = block_of(flipped_1, signal_1, at, -1, False, shards)


def settle_kernel(kept, within, crossed, missing, within_back, crossed_back, current_in, cotangent_in):
    current_in[...] = entering(kept, within, crossed)
    cotangent_in[...] = turning(missing, within_back, crossed_back)


def sum_of(*values):
    total = values[0].astype(F32)
    for value in values[1:]:
        total = total + value.astype(F32)
    return total


def relay_kernel(far, from_far, relay_0, relay_1):
    relay_0[...] = sum_of(far[0], from_far[0]).astype(BF16)
    relay_1[...] = sum_of(far[1], from_far[1]).astype(BF16)


def across_kernel(shards, ox, before, after, flipped_0, flipped_1, signal_0, signal_1, across, d0, u1):
    at = lax.axis_index("dp")
    across[...] = sum_of(ox[...], before[...], after[...]).astype(BF16)
    d0[...] = block_of(flipped_0, signal_0, at, -1, False, shards)
    u1[...] = block_of(flipped_1, signal_1, at, 1, False, shards)


def onward_kernel(u0, relay_0, d1, relay_1, onward_0, back_1):
    onward_0[...] = sum_of(u0[...], relay_0[...]).astype(BF16)
    back_1[...] = sum_of(d1[...], relay_1[...]).astype(BF16)


def update_kernel(row_scale, weights, momentum, own, across, up_0, up_1, down_0, down_1,
                  new_weights, new_momentum, *rounded):
    for layer_at in range(2):
        total = sum_of(own[layer_at], across[layer_at], (up_0, up_1)[layer_at][...], (down_0, down_1)[layer_at][...])
        moved = momentum_decay * momentum[layer_at] + total * row_scale
        new_momentum[layer_at] = moved
        stepped = weights[layer_at] - learn_rate * moved
        new_weights[layer_at] = stepped
        if rounded:
            rounded[0][layer_at] = stepped.astype(BF16)
            rounded[1 + layer_at][...] = stepped.astype(BF16)


def local(weights, momentum, boundary, adjoint, target):
    shards = lax.axis_size("dp")
    layers, own_rows, width = weights.shape
    rows = boundary.shape[1]
    width_scale = 1.0 / math.sqrt(width)
    row_scale = 1.0 / math.sqrt(rows * shards)
    state = (rows, width)
    shard = (layers, own_rows, width)
    block = (own_rows, width)
    whole = (layers, width, width)
    product = rows * width * width
    kept = boundary[0]
    entered = ()
    returned = (adjoint[0],)
    own = on_device(round_kernel, [(shard, BF16), (block, BF16), (block, BF16)], (weights,))
    for update_at in range(STEPS):
        fresh = update_at == 0
        both, first, second = own
        b0 = turned(first, 1)
        a1 = turned(second, -1)
        b1 = turned(second, 1)
        a0 = turned(first, -1)
        other = swapped(both)
        f0 = turned(b0, 1)
        f1 = turned(a1, -1)
        other_before = turned(other, 1)
        other_after = turned(other, -1)
        partly, far = on_device(
            near_kernel, [(whole, BF16), (shard, BF16)], (both, other, b0, b1, a0, a1, f0, f1),
        )
        partly, current = on_device(
            functools.partial(across_pieces_kernel, fresh), [(whole, BF16), (state, F32)],
            (partly, other_before, other_after, kept, *entered), 0, {0: 0},
        )
        full, outgoing = on_device(
            functools.partial(first_forward_kernel, width_scale), [(whole, BF16), (state, BF16)],
            (partly, swapped(far), current), 4 * product, {0: 0},
        )
        within = passed(outgoing, 1, False)
        crossed = passed(outgoing, 1, True)
        from_within = on_device(
            functools.partial(within_forward_kernel, width_scale), [(state, BF16)], (within, full), 4 * product,
        )[0]
        crossed_last = passed(from_within, 1, True)
        from_crossed = on_device(
            functools.partial(crossed_forward_kernel, width_scale), [(state, BF16)], (kept, crossed, full), 4 * product,
        )[0]
        entered = (passed(from_crossed, 1, False), crossed_last)
        missing, input_0, input_1, bend_0, bend_1, starting = on_device(
            functools.partial(turn_kernel, width_scale, fresh),
            [(state, F32)] + [(state, BF16)] * 2 + [(state, F32)] * 2 + [(state, BF16)],
            (kept, *entered, full, target, *returned), 8 * product,
        )
        bends = (bend_0, bend_1)
        within = passed(starting, -1, False)
        crossed = passed(starting, -1, True)
        flipped = on_device(flip_kernel, [((width, rows), BF16)] * 2, (input_0, input_1))
        from_within = on_device(
            functools.partial(within_backward_kernel, width_scale), [(state, BF16)], (within, full, *bends), 4 * product,
        )[0]
        crossed_last = passed(from_within, -1, True)
        from_crossed = on_device(
            functools.partial(crossed_backward_kernel, width_scale), [(state, BF16)],
            (missing, crossed, full, *bends), 4 * product,
        )[0]
        returned = (missing, passed(from_crossed, -1, False), crossed_last)
        fx, ux, dx, *signals = on_device(
            functools.partial(far_gradient_kernel, width_scale, shards),
            [(shard, BF16)] * 3 + [(state, BF16)] * 2, (*returned, full, *flipped, *bends), 4 * product,
        )
        from_far = swapped(fx)
        before = turned(ux, 1)
        after = turned(dx, -1)
        far, ox, u0, d1, mine = on_device(
            functools.partial(near_gradient_kernel, shards),
            [(shard, BF16)] * 2 + [(block, BF16)] * 2 + [(shard, BF16)], (*flipped, *signals), 2 * product,
        )
        relay_0, relay_1 = on_device(relay_kernel, [(block, BF16)] * 2, (far, from_far))
        relay_0 = turned(relay_0, 1)
        relay_1 = turned(relay_1, -1)
        across, d0, u1 = on_device(
            functools.partial(across_kernel, shards), [(shard, BF16), (block, BF16), (block, BF16)],
            (ox, before, after, *flipped, *signals), product,
        )
        across = swapped(across)
        up_1 = turned(u1, 1)
        down_0 = turned(d0, -1)
        onward_0, back_1 = on_device(onward_kernel, [(block, BF16)] * 2, (u0, relay_0, d1, relay_1))
        rounded = [] if update_at == STEPS - 1 else [(shard, BF16), (block, BF16), (block, BF16)]
        weights, momentum, *own = on_device(
            functools.partial(update_kernel, row_scale), [(shard, F32), (shard, F32), *rounded],
            (weights, momentum, mine, across, turned(onward_0, 1), up_1, down_0, turned(back_1, -1)),
        )
    current_in, cotangent_in = on_device(settle_kernel, [(state, F32)] * 2, (kept, *entered, *returned))
    return (weights, momentum, current_in[None], cotangent_in[None])


def solution(mesh):
    placed = (
        P("layer", "dp", None),
        P("layer", "dp", None),
        P("layer", "dp", None),
        P("layer", "dp", None),
        P("dp", None),
    )
    return jax.shard_map(
        local,
        mesh=mesh,
        in_specs=placed,
        out_specs=(
            P("layer", "dp", None),
            P("layer", "dp", None),
            P("layer", "dp", None),
            P("layer", "dp", None),
        ),
        check_vma=False,
    )
```

```python
import functools
import math

import jax
import jax.numpy as jnp
from jax import lax
from jax.experimental import pallas as pl
from jax.experimental.pallas import tpu as pltpu
from jax.sharding import PartitionSpec as P

STEPS = 2
SWEEPS = 2


step_size = 0.5
momentum_decay = 0.9
learn_rate = 0.05
HALVES = 2
F32 = jnp.float32
BF16 = jnp.bfloat16


def passed(value, by, crossing):
    groups = lax.axis_size("layer")
    pairs = [(i, i + by) for i in range(groups) if 0 <= i + by < groups]
    return lax.ppermute(value, "layer", [(i, j) for i, j in pairs if (i // 2 != j // 2) == crossing])


def turned(value, by):
    shards = lax.axis_size("dp")
    return lax.ppermute(value, "dp", [(i, (i + HALVES * by) % shards) for i in range(shards)])


def swapped(value):
    shards = lax.axis_size("dp")
    return lax.ppermute(value, "dp", [(i, i ^ 1) for i in range(shards)])


def on_device(body, outs, operands, flops=0, in_place=None):
    whole = pl.BlockSpec(memory_space=pltpu.VMEM)
    shapes = [jax.ShapeDtypeStruct(shape, kind) for shape, kind in outs]
    moved = sum(math.prod(o.shape) * o.dtype.itemsize for o in [*operands, *shapes])
    return pl.pallas_call(
        body,
        out_shape=shapes,
        in_specs=[whole] * len(operands),
        out_specs=[whole] * len(shapes),
        input_output_aliases=in_place or {},
        cost_estimate=pl.CostEstimate(flops=flops, bytes_accessed=moved, transcendentals=0),
        compiler_params=pltpu.CompilerParams(vmem_limit_bytes=20 * 2**20),
    )(*operands)


def rows_of(at, turns, across, rows, shards):
    place = lax.rem(at + HALVES * turns + shards, shards)
    if across:
        place = place + 1 - 2 * lax.rem(place, 2)
    return pl.ds(pl.multiple_of(place * rows, rows), rows)


def times(left, right):
    return jnp.dot(left, right, preferred_element_type=F32)


def pull_back(signal, matrix):
    return lax.dot_general(signal, matrix, (((1,), (1,)), ((), ())), preferred_element_type=F32)


def round_kernel(weights, both, first, second):
    rounded = weights[...].astype(BF16)
    both[...] = rounded
    first[...] = rounded[0]
    second[...] = rounded[1]


def layers_forward(current, full, width_scale, inputs=(), bends=()):
    for layer_at in range(full.shape[0]):
        rounded = current.astype(BF16)
        squashed = jnp.tanh(times(rounded, full[layer_at]) * width_scale)
        current = current + step_size * squashed
        if inputs:
            inputs[layer_at][...] = rounded
            bends[layer_at][...] = 1.0 - squashed * squashed
    return current


def layers_backward(cotangent, full, bends, width_scale):
    for layer_at in reversed(range(full.shape[0])):
        signal = (cotangent * bends[layer_at][...]).astype(BF16)
        cotangent = cotangent + step_size * width_scale * pull_back(signal, full[layer_at])
    return cotangent


def entering(kept, within, crossed):
    at = lax.axis_index("layer")
    arrived = jnp.where(lax.rem(at, 2) == 1, within[...], crossed[...])
    return jnp.where(at == 0, kept[...], arrived.astype(F32))


def turning(missing, within, crossed):
    at = lax.axis_index("layer")
    arrived = jnp.where(lax.rem(at, 2) == 0, within[...], crossed[...])
    return jnp.where(at == lax.axis_size("layer") - 1, missing[...], arrived.astype(F32))


def near_kernel(own, other, b0, b1, a0, a1, f0, f1, full, far):
    at = lax.axis_index("dp")
    shards = lax.axis_size("dp")
    rows = own.shape[1]
    for layer_at in range(2):
        def put(piece, turns, across):
            full[layer_at, rows_of(at, turns, across, rows, shards)] = piece

        put(own[layer_at], 0, False)
        put(other[layer_at], 0, True)
        put((b0, b1)[layer_at][...], -1, False)
        put((a0, a1)[layer_at][...], 1, False)
        piece = (f0, f1)[layer_at][...]
        put(piece, 2, False)
        far[layer_at] = piece


def later_kernel(first, second, b0, a1, later_first, later_second):
    later_first[...] = first[...]
    later_second[...] = second[...]


def across_pieces_kernel(fresh, partly, before, after, kept, *refs):
    full, current = refs[-2:]
    at = lax.axis_index("dp")
    shards = lax.axis_size("dp")
    rows = before.shape[1]
    for layer_at in range(2):
        for piece, turns in ((before, -1), (after, 1)):
            full[layer_at, rows_of(at, turns, True, rows, shards)] = piece[layer_at]
    current[...] = kept[...] if fresh else entering(kept, *refs[:2])


def first_forward_kernel(width_scale, partly, far, current, full, outgoing):
    at = lax.axis_index("dp")
    rows = far.shape[1]
    for layer_at in range(2):
        full[layer_at, rows_of(at, 2, True, rows, lax.axis_size("dp"))] = far[layer_at]
    outgoing[...] = layers_forward(current[...], full, width_scale).astype(BF16)


def within_forward_kernel(width_scale, received, full, outgoing):
    outgoing[...] = layers_forward(received[...].astype(F32), full, width_scale).astype(BF16)


def crossed_forward_kernel(width_scale, kept, received, full, outgoing):
    current = jnp.where(lax.axis_index("layer") == 0, kept[...], received[...].astype(F32))
    outgoing[...] = layers_forward(current, full, width_scale).astype(BF16)


def turn_kernel(width_scale, fresh, kept, within, crossed, full, target, *refs):
    if fresh:
        adjoint, *refs = refs
        cotangent = adjoint[...]
    else:
        ending, within_back, crossed_back, *refs = refs
        cotangent = turning(ending, within_back, crossed_back)
    missing, input_0, input_1, bend_0, bend_1, starting = refs
    bends = (bend_0, bend_1)
    finals = layers_forward(entering(kept, within, crossed), full, width_scale, (input_0, input_1), bends)
    missing[...] = finals - target[...]
    starting[...] = layers_backward(cotangent, full, bends, width_scale).astype(BF16)


def within_backward_kernel(width_scale, received, full, bend_0, bend_1, starting):
    starting[...] = layers_backward(received[...].astype(F32), full, (bend_0, bend_1), width_scale).astype(BF16)


def crossed_backward_kernel(width_scale, missing, received, full, bend_0, bend_1, starting):
    last = lax.axis_index("layer") == lax.axis_size("layer") - 1
    cotangent = jnp.where(last, missing[...], received[...].astype(F32))
    starting[...] = layers_backward(cotangent, full, (bend_0, bend_1), width_scale).astype(BF16)


def flip_kernel(input_0, input_1, flipped_0, flipped_1):
    flipped_0[...] = input_0[...].T
    flipped_1[...] = input_1[...].T


def block_of(flipped, signal, at, turns, across, shards):
    rows = flipped.shape[0] // shards
    return times(flipped[rows_of(at, turns, across, rows, shards)], signal[...]).astype(BF16)


def far_gradient_kernel(width_scale, shards, missing, within, crossed, full, flipped_0, flipped_1, bend_0, bend_1,
                        fx, ux, dx, signal_0, signal_1):
    at = lax.axis_index("dp")
    cotangent = turning(missing, within, crossed)
    signal_1[...] = (cotangent * bend_1[...]).astype(BF16)
    cotangent = cotangent + step_size * width_scale * pull_back(signal_1[...], full[1])
    signal_0[...] = (cotangent * bend_0[...]).astype(BF16)
    for layer_at, flipped, signal in ((0, flipped_0, signal_0), (1, flipped_1, signal_1)):
        fx[layer_at] = block_of(flipped, signal, at, 2, True, shards)
        ux[layer_at] = block_of(flipped, signal, at, 1, True, shards)
        dx[layer_at] = block_of(flipped, signal, at, -1, True, shards)


def near_gradient_kernel(shards, flipped_0, flipped_1, signal_0, signal_1, far, ox, u0, d1, own):
    at = lax.axis_index("dp")
    for layer_at, flipped, signal in ((0, flipped_0, signal_0), (1, flipped_1, signal_1)):
        far[layer_at] = block_of(flipped, signal, at, 2, False, shards)
        ox[layer_at] = block_of(flipped, signal, at, 0, True, shards)
        own[layer_at] = block_of(flipped, signal, at, 0, False, shards)
    u0[...] = block_of(flipped_0, signal_0, at, 1, False, shards)
    d1[...] = block_of(flipped_1, signal_1, at, -1, False, shards)


def settle_kernel(kept, within, crossed, missing, within_back, crossed_back, current_in, cotangent_in):
    current_in[...] = entering(kept, within, crossed)
    cotangent_in[...] = turning(missing, within_back, crossed_back)


def sum_of(*values):
    total = values[0].astype(F32)
    for value in values[1:]:
        total = total + value.astype(F32)
    return total


def relay_kernel(far, from_far, relay_0, relay_1):
    relay_0[...] = sum_of(far[0], from_far[0]).astype(BF16)
    relay_1[...] = sum_of(far[1], from_far[1]).astype(BF16)


def across_kernel(shards, ox, before, after, flipped_0, flipped_1, signal_0, signal_1, across, d0, u1):
    at = lax.axis_index("dp")
    across[...] = sum_of(ox[...], before[...], after[...]).astype(BF16)
    d0[...] = block_of(flipped_0, signal_0, at, -1, False, shards)
    u1[...] = block_of(flipped_1, signal_1, at, 1, False, shards)


def onward_kernel(u0, relay_0, d1, relay_1, onward_0, back_1):
    onward_0[...] = sum_of(u0[...], relay_0[...]).astype(BF16)
    back_1[...] = sum_of(d1[...], relay_1[...]).astype(BF16)


def update_kernel(row_scale, weights, momentum, own, across, up_0, up_1, down_0, down_1,
                  new_weights, new_momentum, *rounded):
    for layer_at in range(2):
        total = sum_of(own[layer_at], across[layer_at], (up_0, up_1)[layer_at][...], (down_0, down_1)[layer_at][...])
        moved = momentum_decay * momentum[layer_at] + total * row_scale
        new_momentum[layer_at] = moved
        stepped = weights[layer_at] - learn_rate * moved
        new_weights[layer_at] = stepped
        if rounded:
            rounded[0][layer_at] = stepped.astype(BF16)
            rounded[1 + layer_at][...] = stepped.astype(BF16)


def local(weights, momentum, boundary, adjoint, target):
    shards = lax.axis_size("dp")
    layers, own_rows, width = weights.shape
    rows = boundary.shape[1]
    width_scale = 1.0 / math.sqrt(width)
    row_scale = 1.0 / math.sqrt(rows * shards)
    state = (rows, width)
    shard = (layers, own_rows, width)
    block = (own_rows, width)
    whole = (layers, width, width)
    product = rows * width * width
    kept = boundary[0]
    entered = ()
    returned = (adjoint[0],)
    own = on_device(round_kernel, [(shard, BF16), (block, BF16), (block, BF16)], (weights,))
    for update_at in range(STEPS):
        fresh = update_at == 0
        both, first, second = own
        b0 = turned(first, 1)
        a1 = turned(second, -1)
        other = swapped(both)
        f0 = turned(b0, 1)
        f1 = turned(a1, -1)
        later_first, later_second = on_device(later_kernel, [(block, BF16)] * 2, (first, second, b0, a1))
        b1 = turned(later_second, 1)
        a0 = turned(later_first, -1)
        other_before = turned(other, 1)
        other_after = turned(other, -1)
        partly, far = on_device(
            near_kernel, [(whole, BF16), (shard, BF16)], (both, other, b0, b1, a0, a1, f0, f1),
        )
        partly, current = on_device(
            functools.partial(across_pieces_kernel, fresh), [(whole, BF16), (state, F32)],
            (partly, other_before, other_after, kept, *entered), 0, {0: 0},
        )
        full, outgoing = on_device(
            functools.partial(first_forward_kernel, width_scale), [(whole, BF16), (state, BF16)],
            (partly, swapped(far), current), 4 * product, {0: 0},
        )
        within = passed(outgoing, 1, False)
        crossed = passed(outgoing, 1, True)
        from_within = on_device(
            functools.partial(within_forward_kernel, width_scale), [(state, BF16)], (within, full), 4 * product,
        )[0]
        crossed_last = passed(from_within, 1, True)
        from_crossed = on_device(
            functools.partial(crossed_forward_kernel, width_scale), [(state, BF16)], (kept, crossed, full), 4 * product,
        )[0]
        entered = (passed(from_crossed, 1, False), crossed_last)
        missing, input_0, input_1, bend_0, bend_1, starting = on_device(
            functools.partial(turn_kernel, width_scale, fresh),
            [(state, F32)] + [(state, BF16)] * 2 + [(state, F32)] * 2 + [(state, BF16)],
            (kept, *entered, full, target, *returned), 8 * product,
        )
        bends = (bend_0, bend_1)
        within = passed(starting, -1, False)
        crossed = passed(starting, -1, True)
        flipped = on_device(flip_kernel, [((width, rows), BF16)] * 2, (input_0, input_1))
        from_within = on_device(
            functools.partial(within_backward_kernel, width_scale), [(state, BF16)], (within, full, *bends), 4 * product,
        )[0]
        crossed_last = passed(from_within, -1, True)
        from_crossed = on_device(
            functools.partial(crossed_backward_kernel, width_scale), [(state, BF16)],
            (missing, crossed, full, *bends), 4 * product,
        )[0]
        returned = (missing, passed(from_crossed, -1, False), crossed_last)
        fx, ux, dx, *signals = on_device(
            functools.partial(far_gradient_kernel, width_scale, shards),
            [(shard, BF16)] * 3 + [(state, BF16)] * 2, (*returned, full, *flipped, *bends), 4 * product,
        )
        from_far = swapped(fx)
        before = turned(ux, 1)
        after = turned(dx, -1)
        far, ox, u0, d1, mine = on_device(
            functools.partial(near_gradient_kernel, shards),
            [(shard, BF16)] * 2 + [(block, BF16)] * 2 + [(shard, BF16)], (*flipped, *signals), 2 * product,
        )
        relay_0, relay_1 = on_device(relay_kernel, [(block, BF16)] * 2, (far, from_far))
        relay_0 = turned(relay_0, 1)
        relay_1 = turned(relay_1, -1)
        across, d0, u1 = on_device(
            functools.partial(across_kernel, shards), [(shard, BF16), (block, BF16), (block, BF16)],
            (ox, before, after, *flipped, *signals), product,
        )
        across = swapped(across)
        up_1 = turned(u1, 1)
        down_0 = turned(d0, -1)
        onward_0, back_1 = on_device(onward_kernel, [(block, BF16)] * 2, (u0, relay_0, d1, relay_1))
        rounded = [] if update_at == STEPS - 1 else [(shard, BF16), (block, BF16), (block, BF16)]
        weights, momentum, *own = on_device(
            functools.partial(update_kernel, row_scale), [(shard, F32), (shard, F32), *rounded],
            (weights, momentum, mine, across, turned(onward_0, 1), up_1, down_0, turned(back_1, -1)),
        )
    current_in, cotangent_in = on_device(settle_kernel, [(state, F32)] * 2, (kept, *entered, *returned))
    return (weights, momentum, current_in[None], cotangent_in[None])


def solution(mesh):
    placed = (
        P("layer", "dp", None),
        P("layer", "dp", None),
        P("layer", "dp", None),
        P("layer", "dp", None),
        P("dp", None),
    )
    return jax.shard_map(
        local,
        mesh=mesh,
        in_specs=placed,
        out_specs=(
            P("layer", "dp", None),
            P("layer", "dp", None),
            P("layer", "dp", None),
            P("layer", "dp", None),
        ),
        check_vma=False,
    )
```

```python
import functools
import math

import jax
import jax.numpy as jnp
from jax import lax
from jax.experimental import pallas as pl
from jax.experimental.pallas import tpu as pltpu
from jax.sharding import PartitionSpec as P

STEPS = 2
SWEEPS = 2


step_size = 0.5
momentum_decay = 0.9
learn_rate = 0.05
HALVES = 2
F32 = jnp.float32
BF16 = jnp.bfloat16


def passed(value, by, crossing):
    groups = lax.axis_size("layer")
    pairs = [(i, i + by) for i in range(groups) if 0 <= i + by < groups]
    return lax.ppermute(value, "layer", [(i, j) for i, j in pairs if (i // 2 != j // 2) == crossing])


def turned(value, by):
    shards = lax.axis_size("dp")
    return lax.ppermute(value, "dp", [(i, (i + HALVES * by) % shards) for i in range(shards)])


def swapped(value):
    shards = lax.axis_size("dp")
    return lax.ppermute(value, "dp", [(i, i ^ 1) for i in range(shards)])


def on_device(body, outs, operands, flops=0, in_place=None):
    whole = pl.BlockSpec(memory_space=pltpu.VMEM)
    shapes = [jax.ShapeDtypeStruct(shape, kind) for shape, kind in outs]
    moved = sum(math.prod(o.shape) * o.dtype.itemsize for o in [*operands, *shapes])
    return pl.pallas_call(
        body,
        out_shape=shapes,
        in_specs=[whole] * len(operands),
        out_specs=[whole] * len(shapes),
        input_output_aliases=in_place or {},
        cost_estimate=pl.CostEstimate(flops=flops, bytes_accessed=moved, transcendentals=0),
        compiler_params=pltpu.CompilerParams(vmem_limit_bytes=20 * 2**20),
    )(*operands)


def rows_of(at, turns, across, rows, shards):
    place = lax.rem(at + HALVES * turns + shards, shards)
    if across:
        place = place + 1 - 2 * lax.rem(place, 2)
    return pl.ds(pl.multiple_of(place * rows, rows), rows)


def times(left, right):
    return jnp.dot(left, right, preferred_element_type=F32)


def pull_back(signal, matrix):
    return lax.dot_general(signal, matrix, (((1,), (1,)), ((), ())), preferred_element_type=F32)


def round_kernel(weights, both, first, second):
    rounded = weights[...].astype(BF16)
    both[...] = rounded
    first[...] = rounded[0]
    second[...] = rounded[1]


def layers_forward(current, full, width_scale, inputs=(), bends=()):
    for layer_at in range(full.shape[0]):
        rounded = current.astype(BF16)
        squashed = jnp.tanh(times(rounded, full[layer_at]) * width_scale)
        current = current + step_size * squashed
        if inputs:
            inputs[layer_at][...] = rounded
            bends[layer_at][...] = 1.0 - squashed * squashed
    return current


def layers_backward(cotangent, full, bends, width_scale):
    for layer_at in reversed(range(full.shape[0])):
        signal = (cotangent * bends[layer_at][...]).astype(BF16)
        cotangent = cotangent + step_size * width_scale * pull_back(signal, full[layer_at])
    return cotangent


def entering(kept, within, crossed):
    at = lax.axis_index("layer")
    arrived = jnp.where(lax.rem(at, 2) == 1, within[...], crossed[...])
    return jnp.where(at == 0, kept[...], arrived.astype(F32))


def turning(missing, within, crossed):
    at = lax.axis_index("layer")
    arrived = jnp.where(lax.rem(at, 2) == 0, within[...], crossed[...])
    return jnp.where(at == lax.axis_size("layer") - 1, missing[...], arrived.astype(F32))


def near_kernel(own, other, b0, b1, a0, a1, f0, f1, full, far):
    at = lax.axis_index("dp")
    shards = lax.axis_size("dp")
    rows = own.shape[1]
    for layer_at in range(2):
        def put(piece, turns, across):
            full[layer_at, rows_of(at, turns, across, rows, shards)] = piece

        put(own[layer_at], 0, False)
        put(other[layer_at], 0, True)
        put((b0, b1)[layer_at][...], -1, False)
        put((a0, a1)[layer_at][...], 1, False)
        piece = (f0, f1)[layer_at][...]
        put(piece, 2, False)
        far[layer_at] = piece


def across_pieces_kernel(fresh, partly, before, after, kept, *refs):
    full, current = refs[-2:]
    at = lax.axis_index("dp")
    shards = lax.axis_size("dp")
    rows = before.shape[1]
    for layer_at in range(2):
        for piece, turns in ((before, -1), (after, 1)):
            full[layer_at, rows_of(at, turns, True, rows, shards)] = piece[layer_at]
    current[...] = kept[...] if fresh else entering(kept, *refs[:2])


def first_forward_kernel(width_scale, partly, far, current, full, outgoing):
    at = lax.axis_index("dp")
    rows = far.shape[1]
    for layer_at in range(2):
        full[layer_at, rows_of(at, 2, True, rows, lax.axis_size("dp"))] = far[layer_at]
    outgoing[...] = layers_forward(current[...], full, width_scale).astype(BF16)


def within_forward_kernel(width_scale, received, full, outgoing):
    outgoing[...] = layers_forward(received[...].astype(F32), full, width_scale).astype(BF16)


def crossed_forward_kernel(width_scale, kept, received, full, outgoing):
    current = jnp.where(lax.axis_index("layer") == 0, kept[...], received[...].astype(F32))
    outgoing[...] = layers_forward(current, full, width_scale).astype(BF16)


def turn_kernel(width_scale, fresh, kept, within, crossed, full, target, *refs):
    if fresh:
        adjoint, *refs = refs
        cotangent = adjoint[...]
    else:
        ending, within_back, crossed_back, *refs = refs
        cotangent = turning(ending, within_back, crossed_back)
    missing, input_0, input_1, bend_0, bend_1, starting = refs
    bends = (bend_0, bend_1)
    finals = layers_forward(entering(kept, within, crossed), full, width_scale, (input_0, input_1), bends)
    missing[...] = finals - target[...]
    starting[...] = layers_backward(cotangent, full, bends, width_scale).astype(BF16)


def within_backward_kernel(width_scale, received, full, bend_0, bend_1, starting):
    starting[...] = layers_backward(received[...].astype(F32), full, (bend_0, bend_1), width_scale).astype(BF16)


def crossed_backward_kernel(width_scale, missing, received, full, bend_0, bend_1, starting):
    last = lax.axis_index("layer") == lax.axis_size("layer") - 1
    cotangent = jnp.where(last, missing[...], received[...].astype(F32))
    starting[...] = layers_backward(cotangent, full, (bend_0, bend_1), width_scale).astype(BF16)


def flip_kernel(input_0, input_1, flipped_0, flipped_1):
    flipped_0[...] = input_0[...].T
    flipped_1[...] = input_1[...].T


def block_of(flipped, signal, at, turns, across, shards):
    rows = flipped.shape[0] // shards
    return times(flipped[rows_of(at, turns, across, rows, shards)], signal[...]).astype(BF16)


def far_gradient_kernel(width_scale, shards, missing, within, crossed, full, flipped_0, flipped_1, bend_0, bend_1,
                        fx, signal_0, signal_1):
    at = lax.axis_index("dp")
    cotangent = turning(missing, within, crossed)
    signal_1[...] = (cotangent * bend_1[...]).astype(BF16)
    fx[1] = block_of(flipped_1, signal_1, at, 2, True, shards)
    cotangent = cotangent + step_size * width_scale * pull_back(signal_1[...], full[1])
    signal_0[...] = (cotangent * bend_0[...]).astype(BF16)
    fx[0] = block_of(flipped_0, signal_0, at, 2, True, shards)


def side_gradient_kernel(shards, flipped_0, flipped_1, signal_0, signal_1, ux, dx):
    at = lax.axis_index("dp")
    for layer_at, flipped, signal in ((0, flipped_0, signal_0), (1, flipped_1, signal_1)):
        ux[layer_at] = block_of(flipped, signal, at, 1, True, shards)
        dx[layer_at] = block_of(flipped, signal, at, -1, True, shards)


def near_gradient_kernel(shards, flipped_0, flipped_1, signal_0, signal_1, far, ox, u0, d1, own):
    at = lax.axis_index("dp")
    for layer_at, flipped, signal in ((0, flipped_0, signal_0), (1, flipped_1, signal_1)):
        far[layer_at] = block_of(flipped, signal, at, 2, False, shards)
        ox[layer_at] = block_of(flipped, signal, at, 0, True, shards)
        own[layer_at] = block_of(flipped, signal, at, 0, False, shards)
    u0[...] = block_of(flipped_0, signal_0, at, 1, False, shards)
    d1[...] = block_of(flipped_1, signal_1, at, -1, False, shards)


def settle_kernel(kept, within, crossed, missing, within_back, crossed_back, current_in, cotangent_in):
    current_in[...] = entering(kept, within, crossed)
    cotangent_in[...] = turning(missing, within_back, crossed_back)


def sum_of(*values):
    total = values[0].astype(F32)
    for value in values[1:]:
        total = total + value.astype(F32)
    return total


def relay_kernel(far, from_far, relay_0, relay_1):
    relay_0[...] = sum_of(far[0], from_far[0]).astype(BF16)
    relay_1[...] = sum_of(far[1], from_far[1]).astype(BF16)


def across_kernel(shards, ox, before, after, flipped_0, flipped_1, signal_0, signal_1, across, d0, u1):
    at = lax.axis_index("dp")
    across[...] = sum_of(ox[...], before[...], after[...]).astype(BF16)
    d0[...] = block_of(flipped_0, signal_0, at, -1, False, shards)
    u1[...] = block_of(flipped_1, signal_1, at, 1, False, shards)


def onward_kernel(u0, relay_0, d1, relay_1, onward_0, back_1):
    onward_0[...] = sum_of(u0[...], relay_0[...]).astype(BF16)
    back_1[...] = sum_of(d1[...], relay_1[...]).astype(BF16)


def update_kernel(row_scale, weights, momentum, own, across, up_0, up_1, down_0, down_1,
                  new_weights, new_momentum, *rounded):
    for layer_at in range(2):
        total = sum_of(own[layer_at], across[layer_at], (up_0, up_1)[layer_at][...], (down_0, down_1)[layer_at][...])
        moved = momentum_decay * momentum[layer_at] + total * row_scale
        new_momentum[layer_at] = moved
        stepped = weights[layer_at] - learn_rate * moved
        new_weights[layer_at] = stepped
        if rounded:
            rounded[0][layer_at] = stepped.astype(BF16)
            rounded[1 + layer_at][...] = stepped.astype(BF16)


def local(weights, momentum, boundary, adjoint, target):
    shards = lax.axis_size("dp")
    layers, own_rows, width = weights.shape
    rows = boundary.shape[1]
    width_scale = 1.0 / math.sqrt(width)
    row_scale = 1.0 / math.sqrt(rows * shards)
    state = (rows, width)
    shard = (layers, own_rows, width)
    block = (own_rows, width)
    whole = (layers, width, width)
    product = rows * width * width
    kept = boundary[0]
    entered = ()
    returned = (adjoint[0],)
    own = on_device(round_kernel, [(shard, BF16), (block, BF16), (block, BF16)], (weights,))
    for update_at in range(STEPS):
        fresh = update_at == 0
        both, first, second = own
        b0 = turned(first, 1)
        a1 = turned(second, -1)
        b1 = turned(second, 1)
        a0 = turned(first, -1)
        other = swapped(both)
        f0 = turned(b0, 1)
        f1 = turned(a1, -1)
        other_before = turned(other, 1)
        other_after = turned(other, -1)
        partly, far = on_device(
            near_kernel, [(whole, BF16), (shard, BF16)], (both, other, b0, b1, a0, a1, f0, f1),
        )
        partly, current = on_device(
            functools.partial(across_pieces_kernel, fresh), [(whole, BF16), (state, F32)],
            (partly, other_before, other_after, kept, *entered), 0, {0: 0},
        )
        full, outgoing = on_device(
            functools.partial(first_forward_kernel, width_scale), [(whole, BF16), (state, BF16)],
            (partly, swapped(far), current), 4 * product, {0: 0},
        )
        within = passed(outgoing, 1, False)
        crossed = passed(outgoing, 1, True)
        from_within = on_device(
            functools.partial(within_forward_kernel, width_scale), [(state, BF16)], (within, full), 4 * product,
        )[0]
        crossed_last = passed(from_within, 1, True)
        from_crossed = on_device(
            functools.partial(crossed_forward_kernel, width_scale), [(state, BF16)], (kept, crossed, full), 4 * product,
        )[0]
        entered = (passed(from_crossed, 1, False), crossed_last)
        missing, input_0, input_1, bend_0, bend_1, starting = on_device(
            functools.partial(turn_kernel, width_scale, fresh),
            [(state, F32)] + [(state, BF16)] * 2 + [(state, F32)] * 2 + [(state, BF16)],
            (kept, *entered, full, target, *returned), 8 * product,
        )
        bends = (bend_0, bend_1)
        within = passed(starting, -1, False)
        crossed = passed(starting, -1, True)
        flipped = on_device(flip_kernel, [((width, rows), BF16)] * 2, (input_0, input_1))
        from_within = on_device(
            functools.partial(within_backward_kernel, width_scale), [(state, BF16)], (within, full, *bends), 4 * product,
        )[0]
        crossed_last = passed(from_within, -1, True)
        from_crossed = on_device(
            functools.partial(crossed_backward_kernel, width_scale), [(state, BF16)],
            (missing, crossed, full, *bends), 4 * product,
        )[0]
        returned = (missing, passed(from_crossed, -1, False), crossed_last)
        fx, *signals = on_device(
            functools.partial(far_gradient_kernel, width_scale, shards),
            [(shard, BF16)] + [(state, BF16)] * 2, (*returned, full, *flipped, *bends), 3 * product,
        )
        from_far = swapped(fx)
        ux, dx = on_device(
            functools.partial(side_gradient_kernel, shards), [(shard, BF16)] * 2, (*flipped, *signals), product,
        )
        before = turned(ux, 1)
        after = turned(dx, -1)
        far, ox, u0, d1, mine = on_device(
            functools.partial(near_gradient_kernel, shards),
            [(shard, BF16)] * 2 + [(block, BF16)] * 2 + [(shard, BF16)], (*flipped, *signals), 2 * product,
        )
        relay_0, relay_1 = on_device(relay_kernel, [(block, BF16)] * 2, (far, from_far))
        relay_0 = turned(relay_0, 1)
        relay_1 = turned(relay_1, -1)
        across, d0, u1 = on_device(
            functools.partial(across_kernel, shards), [(shard, BF16), (block, BF16), (block, BF16)],
            (ox, before, after, *flipped, *signals), product,
        )
        across = swapped(across)
        up_1 = turned(u1, 1)
        down_0 = turned(d0, -1)
        onward_0, back_1 = on_device(onward_kernel, [(block, BF16)] * 2, (u0, relay_0, d1, relay_1))
        rounded = [] if update_at == STEPS - 1 else [(shard, BF16), (block, BF16), (block, BF16)]
        weights, momentum, *own = on_device(
            functools.partial(update_kernel, row_scale), [(shard, F32), (shard, F32), *rounded],
            (weights, momentum, mine, across, turned(onward_0, 1), up_1, down_0, turned(back_1, -1)),
        )
    current_in, cotangent_in = on_device(settle_kernel, [(state, F32)] * 2, (kept, *entered, *returned))
    return (weights, momentum, current_in[None], cotangent_in[None])


def solution(mesh):
    placed = (
        P("layer", "dp", None),
        P("layer", "dp", None),
        P("layer", "dp", None),
        P("layer", "dp", None),
        P("dp", None),
    )
    return jax.shard_map(
        local,
        mesh=mesh,
        in_specs=placed,
        out_specs=(
            P("layer", "dp", None),
            P("layer", "dp", None),
            P("layer", "dp", None),
            P("layer", "dp", None),
        ),
        check_vma=False,
    )
```

```python
import functools
import math

import jax
import jax.numpy as jnp
from jax import lax
from jax.experimental import pallas as pl
from jax.experimental.pallas import tpu as pltpu
from jax.sharding import PartitionSpec as P

STEPS = 2
SWEEPS = 2


step_size = 0.5
momentum_decay = 0.9
learn_rate = 0.05
HALVES = 2
F32 = jnp.float32
BF16 = jnp.bfloat16


def passed(value, by, crossing):
    groups = lax.axis_size("layer")
    pairs = [(i, i + by) for i in range(groups) if 0 <= i + by < groups]
    return lax.ppermute(value, "layer", [(i, j) for i, j in pairs if (i // 2 != j // 2) == crossing])


def turned(value, by):
    shards = lax.axis_size("dp")
    return lax.ppermute(value, "dp", [(i, (i + HALVES * by) % shards) for i in range(shards)])


def swapped(value):
    shards = lax.axis_size("dp")
    return lax.ppermute(value, "dp", [(i, i ^ 1) for i in range(shards)])


def on_device(body, outs, operands, flops=0, in_place=None):
    whole = pl.BlockSpec(memory_space=pltpu.VMEM)
    shapes = [jax.ShapeDtypeStruct(shape, kind) for shape, kind in outs]
    moved = sum(math.prod(o.shape) * o.dtype.itemsize for o in [*operands, *shapes])
    return pl.pallas_call(
        body,
        out_shape=shapes,
        in_specs=[whole] * len(operands),
        out_specs=[whole] * len(shapes),
        input_output_aliases=in_place or {},
        cost_estimate=pl.CostEstimate(flops=flops, bytes_accessed=moved, transcendentals=0),
        compiler_params=pltpu.CompilerParams(vmem_limit_bytes=20 * 2**20),
    )(*operands)


def rows_of(at, turns, across, rows, shards):
    place = lax.rem(at + HALVES * turns + shards, shards)
    if across:
        place = place + 1 - 2 * lax.rem(place, 2)
    return pl.ds(pl.multiple_of(place * rows, rows), rows)


def times(left, right):
    return jnp.dot(left, right, preferred_element_type=F32)


def pull_back(signal, matrix):
    return lax.dot_general(signal, matrix, (((1,), (1,)), ((), ())), preferred_element_type=F32)


def round_kernel(weights, both, first, second):
    rounded = weights[...].astype(BF16)
    both[...] = rounded
    first[...] = rounded[0]
    second[...] = rounded[1]


def layers_forward(current, full, width_scale, inputs=(), bends=()):
    for layer_at in range(full.shape[0]):
        rounded = current.astype(BF16)
        squashed = jnp.tanh(times(rounded, full[layer_at]) * width_scale)
        current = current + step_size * squashed
        if inputs:
            inputs[layer_at][...] = rounded
            bends[layer_at][...] = 1.0 - squashed * squashed
    return current


def layers_backward(cotangent, full, bends, width_scale):
    for layer_at in reversed(range(full.shape[0])):
        signal = (cotangent * bends[layer_at][...]).astype(BF16)
        cotangent = cotangent + step_size * width_scale * pull_back(signal, full[layer_at])
    return cotangent


def entering(kept, within, crossed):
    at = lax.axis_index("layer")
    arrived = jnp.where(lax.rem(at, 2) == 1, within[...], crossed[...])
    return jnp.where(at == 0, kept[...], arrived.astype(F32))


def turning(missing, within, crossed):
    at = lax.axis_index("layer")
    arrived = jnp.where(lax.rem(at, 2) == 0, within[...], crossed[...])
    return jnp.where(at == lax.axis_size("layer") - 1, missing[...], arrived.astype(F32))


def near_kernel(own, other, b0, b1, a0, a1, f0, f1, full, far):
    at = lax.axis_index("dp")
    shards = lax.axis_size("dp")
    rows = own.shape[1]
    for layer_at in range(2):
        def put(piece, turns, across):
            full[layer_at, rows_of(at, turns, across, rows, shards)] = piece

        put(own[layer_at], 0, False)
        put(other[layer_at], 0, True)
        put((b0, b1)[layer_at][...], -1, False)
        put((a0, a1)[layer_at][...], 1, False)
        piece = (f0, f1)[layer_at][...]
        put(piece, 2, False)
        far[layer_at] = piece


def across_pieces_kernel(fresh, partly, before, after, kept, *refs):
    full, current = refs[-2:]
    at = lax.axis_index("dp")
    shards = lax.axis_size("dp")
    rows = before.shape[1]
    for layer_at in range(2):
        for piece, turns in ((before, -1), (after, 1)):
            full[layer_at, rows_of(at, turns, True, rows, shards)] = piece[layer_at]
    current[...] = kept[...] if fresh else entering(kept, *refs[:2])


def first_forward_kernel(width_scale, partly, far, current, full, outgoing):
    at = lax.axis_index("dp")
    rows = far.shape[1]
    for layer_at in range(2):
        full[layer_at, rows_of(at, 2, True, rows, lax.axis_size("dp"))] = far[layer_at]
    outgoing[...] = layers_forward(current[...], full, width_scale).astype(BF16)


def within_forward_kernel(width_scale, received, full, outgoing):
    outgoing[...] = layers_forward(received[...].astype(F32), full, width_scale).astype(BF16)


def crossed_forward_kernel(width_scale, kept, received, full, outgoing):
    current = jnp.where(lax.axis_index("layer") == 0, kept[...], received[...].astype(F32))
    outgoing[...] = layers_forward(current, full, width_scale).astype(BF16)


def turn_kernel(width_scale, fresh, kept, within, crossed, full, target, *refs):
    if fresh:
        adjoint, *refs = refs
        cotangent = adjoint[...]
    else:
        ending, within_back, crossed_back, *refs = refs
        cotangent = turning(ending, within_back, crossed_back)
    missing, input_0, input_1, bend_0, bend_1, starting = refs
    bends = (bend_0, bend_1)
    finals = layers_forward(entering(kept, within, crossed), full, width_scale, (input_0, input_1), bends)
    missing[...] = finals - target[...]
    starting[...] = layers_backward(cotangent, full, bends, width_scale).astype(BF16)


def within_backward_kernel(width_scale, received, full, bend_0, bend_1, starting):
    starting[...] = layers_backward(received[...].astype(F32), full, (bend_0, bend_1), width_scale).astype(BF16)


def crossed_backward_kernel(width_scale, missing, received, full, bend_0, bend_1, starting):
    last = lax.axis_index("layer") == lax.axis_size("layer") - 1
    cotangent = jnp.where(last, missing[...], received[...].astype(F32))
    starting[...] = layers_backward(cotangent, full, (bend_0, bend_1), width_scale).astype(BF16)


def flip_kernel(input_0, input_1, flipped_0, flipped_1):
    flipped_0[...] = input_0[...].T
    flipped_1[...] = input_1[...].T


def block_of(flipped, signal, at, turns, across, shards):
    rows = flipped.shape[0] // shards
    return times(flipped[rows_of(at, turns, across, rows, shards)], signal[...]).astype(BF16)


def far_gradient_kernel(width_scale, shards, missing, within, crossed, full, flipped_0, flipped_1, bend_0, bend_1,
                        fx, signal_0, signal_1):
    at = lax.axis_index("dp")
    cotangent = turning(missing, within, crossed)
    signal_1[...] = (cotangent * bend_1[...]).astype(BF16)
    fx[1] = block_of(flipped_1, signal_1, at, 2, True, shards)
    cotangent = cotangent + step_size * width_scale * pull_back(signal_1[...], full[1])
    signal_0[...] = (cotangent * bend_0[...]).astype(BF16)
    fx[0] = block_of(flipped_0, signal_0, at, 2, True, shards)


def side_gradient_kernel(shards, flipped_0, flipped_1, signal_0, signal_1, ux, dx):
    at = lax.axis_index("dp")
    for layer_at, flipped, signal in ((0, flipped_0, signal_0), (1, flipped_1, signal_1)):
        ux[layer_at] = block_of(flipped, signal, at, 1, True, shards)
        dx[layer_at] = block_of(flipped, signal, at, -1, True, shards)


def near_gradient_kernel(shards, flipped_0, flipped_1, signal_0, signal_1, far, ox, u0, d1, own):
    at = lax.axis_index("dp")
    for layer_at, flipped, signal in ((0, flipped_0, signal_0), (1, flipped_1, signal_1)):
        far[layer_at] = block_of(flipped, signal, at, 2, False, shards)
        ox[layer_at] = block_of(flipped, signal, at, 0, True, shards)
        own[layer_at] = block_of(flipped, signal, at, 0, False, shards)
    u0[...] = block_of(flipped_0, signal_0, at, 1, False, shards)
    d1[...] = block_of(flipped_1, signal_1, at, -1, False, shards)


def settle_kernel(kept, within, crossed, missing, within_back, crossed_back, current_in, cotangent_in):
    current_in[...] = entering(kept, within, crossed)
    cotangent_in[...] = turning(missing, within_back, crossed_back)


def sum_of(*values):
    total = values[0].astype(F32)
    for value in values[1:]:
        total = total + value.astype(F32)
    return total


def relay_kernel(far, from_far, relay_0, relay_1):
    relay_0[...] = sum_of(far[0], from_far[0]).astype(BF16)
    relay_1[...] = sum_of(far[1], from_far[1]).astype(BF16)


def across_kernel(shards, ox, before, after, flipped_0, flipped_1, signal_0, signal_1, across, d0, u1):
    at = lax.axis_index("dp")
    across[...] = sum_of(ox[...], before[...], after[...]).astype(BF16)
    d0[...] = block_of(flipped_0, signal_0, at, -1, False, shards)
    u1[...] = block_of(flipped_1, signal_1, at, 1, False, shards)


def onward_kernel(block, relay, onward):
    onward[...] = sum_of(block[...], relay[...]).astype(BF16)


def update_kernel(row_scale, weights, momentum, own, across, up_0, up_1, down_0, down_1,
                  new_weights, new_momentum, *rounded):
    for layer_at in range(2):
        total = sum_of(own[layer_at], across[layer_at], (up_0, up_1)[layer_at][...], (down_0, down_1)[layer_at][...])
        moved = momentum_decay * momentum[layer_at] + total * row_scale
        new_momentum[layer_at] = moved
        stepped = weights[layer_at] - learn_rate * moved
        new_weights[layer_at] = stepped
        if rounded:
            rounded[0][layer_at] = stepped.astype(BF16)
            rounded[1 + layer_at][...] = stepped.astype(BF16)


def local(weights, momentum, boundary, adjoint, target):
    shards = lax.axis_size("dp")
    layers, own_rows, width = weights.shape
    rows = boundary.shape[1]
    width_scale = 1.0 / math.sqrt(width)
    row_scale = 1.0 / math.sqrt(rows * shards)
    state = (rows, width)
    shard = (layers, own_rows, width)
    block = (own_rows, width)
    whole = (layers, width, width)
    product = rows * width * width
    kept = boundary[0]
    entered = ()
    returned = (adjoint[0],)
    own = on_device(round_kernel, [(shard, BF16), (block, BF16), (block, BF16)], (weights,))
    for update_at in range(STEPS):
        fresh = update_at == 0
        both, first, second = own
        b0 = turned(first, 1)
        a1 = turned(second, -1)
        b1 = turned(second, 1)
        a0 = turned(first, -1)
        other = swapped(both)
        f0 = turned(b0, 1)
        f1 = turned(a1, -1)
        other_before = turned(other, 1)
        other_after = turned(other, -1)
        partly, far = on_device(
            near_kernel, [(whole, BF16), (shard, BF16)], (both, other, b0, b1, a0, a1, f0, f1),
        )
        partly, current = on_device(
            functools.partial(across_pieces_kernel, fresh), [(whole, BF16), (state, F32)],
            (partly, other_before, other_after, kept, *entered), 0, {0: 0},
        )
        full, outgoing = on_device(
            functools.partial(first_forward_kernel, width_scale), [(whole, BF16), (state, BF16)],
            (partly, swapped(far), current), 4 * product, {0: 0},
        )
        within = passed(outgoing, 1, False)
        crossed = passed(outgoing, 1, True)
        from_within = on_device(
            functools.partial(within_forward_kernel, width_scale), [(state, BF16)], (within, full), 4 * product,
        )[0]
        crossed_last = passed(from_within, 1, True)
        from_crossed = on_device(
            functools.partial(crossed_forward_kernel, width_scale), [(state, BF16)], (kept, crossed, full), 4 * product,
        )[0]
        entered = (passed(from_crossed, 1, False), crossed_last)
        missing, input_0, input_1, bend_0, bend_1, starting = on_device(
            functools.partial(turn_kernel, width_scale, fresh),
            [(state, F32)] + [(state, BF16)] * 2 + [(state, F32)] * 2 + [(state, BF16)],
            (kept, *entered, full, target, *returned), 8 * product,
        )
        bends = (bend_0, bend_1)
        within = passed(starting, -1, False)
        crossed = passed(starting, -1, True)
        flipped = on_device(flip_kernel, [((width, rows), BF16)] * 2, (input_0, input_1))
        from_within = on_device(
            functools.partial(within_backward_kernel, width_scale), [(state, BF16)], (within, full, *bends), 4 * product,
        )[0]
        crossed_last = passed(from_within, -1, True)
        from_crossed = on_device(
            functools.partial(crossed_backward_kernel, width_scale), [(state, BF16)],
            (missing, crossed, full, *bends), 4 * product,
        )[0]
        returned = (missing, passed(from_crossed, -1, False), crossed_last)
        fx, *signals = on_device(
            functools.partial(far_gradient_kernel, width_scale, shards),
            [(shard, BF16)] + [(state, BF16)] * 2, (*returned, full, *flipped, *bends), 3 * product,
        )
        from_far = swapped(fx)
        ux, dx = on_device(
            functools.partial(side_gradient_kernel, shards), [(shard, BF16)] * 2, (*flipped, *signals), product,
        )
        before = turned(ux, 1)
        after = turned(dx, -1)
        far, ox, u0, d1, mine = on_device(
            functools.partial(near_gradient_kernel, shards),
            [(shard, BF16)] * 2 + [(block, BF16)] * 2 + [(shard, BF16)], (*flipped, *signals), 2 * product,
        )
        relay_0, relay_1 = on_device(relay_kernel, [(block, BF16)] * 2, (far, from_far))
        relay_0 = turned(relay_0, 1)
        relay_1 = turned(relay_1, -1)
        across, d0, u1 = on_device(
            functools.partial(across_kernel, shards), [(shard, BF16), (block, BF16), (block, BF16)],
            (ox, before, after, *flipped, *signals), product,
        )
        across = swapped(across)
        up_1 = turned(u1, 1)
        down_0 = turned(d0, -1)
        onward_0, back_1 = [on_device(onward_kernel, [(block, BF16)], pair)[0] for pair in ((u0, relay_0), (d1, relay_1))]
        rounded = [] if update_at == STEPS - 1 else [(shard, BF16), (block, BF16), (block, BF16)]
        weights, momentum, *own = on_device(
            functools.partial(update_kernel, row_scale), [(shard, F32), (shard, F32), *rounded],
            (weights, momentum, mine, across, turned(onward_0, 1), up_1, down_0, turned(back_1, -1)),
        )
    current_in, cotangent_in = on_device(settle_kernel, [(state, F32)] * 2, (kept, *entered, *returned))
    return (weights, momentum, current_in[None], cotangent_in[None])


def solution(mesh):
    placed = (
        P("layer", "dp", None),
        P("layer", "dp", None),
        P("layer", "dp", None),
        P("layer", "dp", None),
        P("dp", None),
    )
    return jax.shard_map(
        local,
        mesh=mesh,
        in_specs=placed,
        out_specs=(
            P("layer", "dp", None),
            P("layer", "dp", None),
            P("layer", "dp", None),
            P("layer", "dp", None),
        ),
        check_vma=False,
    )
```
